32 devices in a mesh: dp: 4 (over x, core), ctx: 4 (over z), rep: 2 (over y).
Axes of the slice: x: 2, y: 2, z: 4, core: 2. Of those that a mesh axis runs over, the one named last changes fastest.
Arguments:
- inputs: bfloat16 [4, 1024, 4096], P('dp', ('ctx', 'rep')), may hold values from -6 to 6
- queries: bfloat16 [4, 1024, 2048], P('dp', ('ctx', 'rep')), may hold values from -24 to 24
- keys: bfloat16 [4, 1024, 512], P('dp', ('ctx', 'rep')), may hold values from -24 to 24
- values: bfloat16 [4, 1024, 512], P('dp', ('ctx', 'rep')), may hold values from -6 to 6
- grad_out: bfloat16 [4, 1024, 2048], P('dp', ('ctx', 'rep')), may hold values from -0.125 to 0.125
- doc_ids: int32 [4, 1024], P('dp', ('ctx', 'rep')), may hold values from 0 to 31, never falling along the last dimension, each value on 1 to 128 neighbouring positions
- plan: int32 [4, 32], P('dp', ('ctx', 'rep')), may hold values from 0 to 3, as said below
Outputs:
- placed_out: bfloat16 [4, 1024, 2048], P('dp', ('ctx', 'rep'))
- weight_grad: float32 [4096, 512], P('ctx')
The draws below stay inside these ranges and needn't reach their ends.
Inputs may be any that keep to these rules, and one draw needn't show every extreme that they name: `doc_ids`: ids never fall along a micro-batch; a document holds at most 128 positions. `plan`: for one sequence shard, the 4 blocks of a micro-batch go to 4 different micro-batches (itself possibly), and every micro-batch receives exactly one block of each local block index.
All inputs are finite; a program needn't handle non-finite values.
Results may differ from the reference program's by a relative error of at most 0.017.
Values may be sent and summed in bfloat16 or wider, within the bound.
No kernel may reach another device: no remote copies, remote signals or barrier semaphores. Data moves between devices by JAX's collectives and lax.ppermute only.
A program may use at most 64 MiB of HBM per device.

```python
import math
import jax
import jax.numpy as jnp
import numpy as np
from jax import lax

D = 4096
HEAD_DIM = 128
Q_HEADS = 16
KV_HEADS = 4
GROUP = 4
TOK_DEV = 128
BLK_DEV = 4
BLOCK = 32
OWNERS = 4
SHARDS = 8
BATCHES = 4
SEQ = 1024
DOCS = 32
DEVICES = 32


def paired_rows(key):
    base_q = jax.random.normal(jax.random.fold_in(key, 101), (BATCHES, SEQ, Q_HEADS * HEAD_DIM), jnp.float32)
    base_k = jax.random.normal(jax.random.fold_in(key, 102), (BATCHES, SEQ, KV_HEADS * HEAD_DIM), jnp.float32)
    base_q = jnp.clip(base_q, -4.5, 4.5)
    base_k = jnp.clip(base_k, -4.5, 4.5)
    return (base_q, base_k)


def draw_queries(key, part):
    return paired_rows(key)[0].astype(jnp.bfloat16)


def draw_keys(key, part):
    return paired_rows(key)[1].astype(jnp.bfloat16)


def draw_plan(key, part):
    groups = SHARDS
    offset_keys = jax.random.split(jax.random.fold_in(key, 201), groups)
    label_keys = jax.random.split(jax.random.fold_in(key, 202), groups)
    offsets = jax.vmap(lambda one_key: jax.random.permutation(one_key, OWNERS)[:BLK_DEV])(offset_keys)
    labels = jax.vmap(lambda one_key: jax.random.permutation(one_key, OWNERS))(label_keys)
    inverse = jnp.argsort(labels, axis=1)
    target = (inverse[:, :, None] + offsets[:, None, :]) % OWNERS
    chosen = jnp.take_along_axis(labels, target.reshape(groups, OWNERS * BLK_DEV), axis=1)
    chosen = chosen.reshape(SHARDS, OWNERS, BLK_DEV)
    chosen = jnp.transpose(chosen, (1, 0, 2)).reshape(BATCHES, SHARDS * BLK_DEV)
    return chosen.astype(jnp.int32)


def raised(result, key, source, target, shards_of, factor):
    owner, partner = [(jnp.arange(result.shape[dim]) // (result.shape[dim] // shards_of)).reshape([-1 if axis == dim else 1 for axis in range(result.ndim)]) for dim in (source, target)]
    chosen = jax.random.permutation(key, shards_of)[partner]
    strong = (owner == chosen) | (owner == (partner + shards_of // 2) % shards_of)
    return jnp.where(strong, factor * result, result)


def block_scale(stream_key, extent, shards, least, high):
    level = 1.0
    for axis_at, shards_of in shards:
        steps = jax.random.uniform(jax.random.fold_in(jax.random.fold_in(stream_key, 6), axis_at), (shards_of,), jnp.float32, least / len(shards), high / len(shards))
        level = level * jnp.repeat(jnp.exp(steps), extent[axis_at] // shards_of).reshape((-1,) + (1,) * (len(extent) - 1 - axis_at))
    return level


def profile(amount, total, reach, lean):
    loads = [(1 << 20) // math.isqrt(rank ** lean) + 1 for rank in range(2, amount + 1)]
    rest, given = total - reach - (amount - 1), [1] * (amount - 1)
    while rest > 0:
        free = [i for i in range(amount - 1) if given[i] < reach]
        whole, left = sum([loads[i] for i in free]), rest
        for i in free:
            addition = min(reach - given[i], max(1, left * loads[i] // whole), rest)
            given[i] = given[i] + addition
            rest = rest - addition
    return np.array([reach] + given)


def ragged_sizes(key, number_of, total, bound, slope):
    if number_of == 2:
        one = jax.random.randint(key, (), max(1, total - bound), min(bound, total - 1) + 1)
        return jnp.stack([one, total - one])
    sizes = jnp.asarray(profile(number_of, total, bound, slope), jnp.int32)
    twos = (number_of - 1) // 2
    source_of, receiver = sizes[1:1 + 2 * twos:2], sizes[2:2 + 2 * twos:2]
    room = jnp.minimum(source_of - 1, bound - receiver)
    moved = jax.random.randint(jax.random.fold_in(key, 1), (twos,), 0, 1 << 20) % (room + 1)
    sizes = sizes.at[1:1 + 2 * twos:2].set(source_of - moved).at[2:2 + 2 * twos:2].set(receiver + moved)
    return sizes[jax.random.permutation(jax.random.fold_in(key, 2), number_of)]


def centred(key, shape, width, bound, shards=(), held_as=jnp.bfloat16):
    entries = jax.random.normal(key, shape, jnp.float32) * width
    if len(shards) > 0:
        entries = block_scale(key, shape, shards, -0.22, 0.18) * entries
    return jnp.clip(entries, min=-bound, max=bound).astype(held_as)


def noise_with(stream_key, shape, width, most, cuts, heavy, held_as=jnp.bfloat16):
    entries = width * jax.random.normal(stream_key, shape, jnp.float32)
    if cuts:
        entries = entries * block_scale(stream_key, shape, cuts, -0.22, 0.18)
    return jnp.clip(raised(entries, jax.random.fold_in(stream_key, 3), *heavy), -most, most).astype(held_as)


def setup_inputs(seed: int = 0) -> dict:
    key_of = jax.random.split(jax.random.key(seed), 8)
    return {
        "inputs": noise_with(key_of[0], (BATCHES, SEQ, D), 1.0, 6.0, ((0, 4), (1, 8)), (1, 2, 8, 2.0)),
        "queries": draw_queries(jax.random.fold_in(key_of[7], 71), 0),
        "keys": draw_keys(jax.random.fold_in(key_of[7], 71), 0),
        "values": centred(key_of[3], (BATCHES, SEQ, KV_HEADS * HEAD_DIM), 1.0, 6.0, ((0, 4), (1, 8))),
        "grad_out": centred(key_of[4], (BATCHES, SEQ, Q_HEADS * HEAD_DIM), (0.5 / (TOK_DEV * DEVICES) ** 0.5), 0.125, ((0, 4), (1, 8))),
        "doc_ids": jax.vmap(lambda own: jnp.searchsorted(jnp.cumsum(ragged_sizes(own, DOCS, SEQ, TOK_DEV, 2)), jnp.arange(SEQ), side="right"))(jax.random.split(key_of[5], BATCHES)).reshape((BATCHES, SEQ)).astype(jnp.int32),
        "plan": draw_plan(jax.random.fold_in(key_of[7], 71), 0),
    }


def shard_weights(query_rows, key_rows, query_docs, key_docs, query_pos, key_pos):
    count_q = query_rows.shape[0]
    count_k = key_rows.shape[0]
    queries4 = query_rows.astype(jnp.float32).reshape(count_q, KV_HEADS, GROUP, HEAD_DIM)
    keys3 = key_rows.astype(jnp.float32).reshape(count_k, KV_HEADS, HEAD_DIM)
    scores = jnp.einsum('tgrd,ugd->grtu', queries4, keys3) * (1.0 / math.sqrt(HEAD_DIM))
    allowed = (query_docs[:, None] == key_docs[None, :]) & (key_pos[None, :] <= query_pos[:, None])
    scores = jnp.where(allowed, scores, -jnp.inf)
    row_max = lax.optimization_barrier(jnp.max(scores, axis=-1, keepdims=True))
    exponent = jnp.exp(scores - row_max)
    row_sum = lax.optimization_barrier(jnp.sum(exponent, axis=-1, keepdims=True))
    return (exponent / row_sum).astype(jnp.bfloat16)

def reference(inputs, queries, keys, values, grad_out, doc_ids, plan):
    q_width = Q_HEADS * HEAD_DIM
    kv_width = KV_HEADS * HEAD_DIM

    def per_batch(grad_sum, batch):
        batch_inputs, batch_queries, batch_keys, batch_values, batch_grads, batch_docs = batch
        keys_pad = jnp.concatenate([jnp.zeros((TOK_DEV, kv_width), batch_keys.dtype), batch_keys], 0)
        values_pad = jnp.concatenate([jnp.zeros((TOK_DEV, kv_width), batch_values.dtype), batch_values], 0)
        docs_pad = jnp.concatenate([jnp.full((TOK_DEV,), -1, jnp.int32), batch_docs], 0)

        def per_shard(shard_index):
            first = shard_index * TOK_DEV
            query_rows = lax.dynamic_slice_in_dim(batch_queries, first, TOK_DEV, 0)
            grad_rows = lax.dynamic_slice_in_dim(batch_grads, first, TOK_DEV, 0)
            query_docs = lax.dynamic_slice_in_dim(batch_docs, first, TOK_DEV, 0)
            key_rows = lax.dynamic_slice_in_dim(keys_pad, first, 2 * TOK_DEV, 0)
            value_rows = lax.dynamic_slice_in_dim(values_pad, first, 2 * TOK_DEV, 0)
            key_docs = lax.dynamic_slice_in_dim(docs_pad, first, 2 * TOK_DEV, 0)
            query_pos = first + jnp.arange(TOK_DEV, dtype=jnp.int32)
            key_pos = first - TOK_DEV + jnp.arange(2 * TOK_DEV, dtype=jnp.int32)
            probabilities = shard_weights(query_rows, key_rows, query_docs, key_docs, query_pos, key_pos)
            weights32 = probabilities.astype(jnp.float32)
            values3 = value_rows.astype(jnp.float32).reshape(2 * TOK_DEV, KV_HEADS, HEAD_DIM)
            attended = jnp.einsum('grtu,ugd->tgrd', weights32, values3).astype(jnp.bfloat16).reshape(TOK_DEV, q_width)
            grads4 = grad_rows.astype(jnp.float32).reshape(TOK_DEV, KV_HEADS, GROUP, HEAD_DIM)
            value_grad = jnp.einsum('grtu,tgrd->ugd', weights32, grads4).reshape(2 * TOK_DEV, kv_width)
            return (attended, value_grad)
        attended, value_grad = lax.map(per_shard, jnp.arange(SHARDS, dtype=jnp.int32))
        own_part = value_grad[:, TOK_DEV:]
        later_part = jnp.concatenate([value_grad[1:, :TOK_DEV], jnp.zeros((1, TOK_DEV, kv_width), value_grad.dtype)], 0)
        grad_values = (own_part + later_part).astype(jnp.bfloat16)

        def per_term(running, pair):
            shard_inputs, shard_grads = pair
            term = jnp.dot(shard_inputs.T, shard_grads, preferred_element_type=jnp.float32)
            rounded = lax.optimization_barrier(term.astype(jnp.bfloat16)).astype(jnp.float32)
            return (running + rounded, None)
        grad_sum, unused = lax.scan(per_term, grad_sum, (batch_inputs.reshape(SHARDS, TOK_DEV, D), grad_values))
        return (grad_sum, attended.reshape(SEQ, q_width))
    weight_grad, attended = lax.scan(per_batch, jnp.zeros((D, kv_width), jnp.float32), (inputs, queries, keys, values, grad_out, doc_ids))
    block_count = SHARDS * BLK_DEV
    pieces = attended.reshape(OWNERS, block_count, BLOCK, q_width)
    targets = plan.reshape(OWNERS, block_count).astype(jnp.int32)
    blk_index = jnp.broadcast_to(jnp.arange(block_count, dtype=jnp.int32)[None, :], targets.shape)
    placed = jnp.zeros_like(pieces).at[targets, blk_index].set(pieces)
    return (placed.reshape(BATCHES, SEQ, q_width), weight_grad)
```

```python
import functools
import math

import jax
import jax.numpy as jnp
from jax import lax
from jax.experimental import pallas as pl
from jax.experimental.pallas import tpu as pltpu
from jax.sharding import PartitionSpec as P

HEAD_DIM = 128
KV_HEADS = 4
GROUP = 4
CORES = 2
LANES = 128
LABEL_ROWS = 16
DOC_BASE = 128
MASKED = -1e30
BF16 = jnp.bfloat16
F32 = jnp.float32


def from_behind(value, axis, by):
    devices = lax.axis_size(axis)
    pairs = [(i, i + by) for i in range(devices) if 0 <= i + by < devices]
    return lax.ppermute(value, axis, pairs)


def swap(value, axis, mask):
    devices = lax.axis_size(axis)
    return lax.ppermute(value, axis, [(i, i ^ mask) for i in range(devices)])


def vmem():
    return pl.BlockSpec(memory_space=pltpu.VMEM)


def smem():
    return pl.BlockSpec(memory_space=pltpu.SMEM)


def call(body, outs, ins, flops=0, limit=None):
    count = sum(math.prod(a.shape) * a.dtype.itemsize for a in (*ins, *outs))
    return pl.pallas_call(
        body,
        out_shape=outs,
        in_specs=[smem() if a.dtype == jnp.int32 and a.ndim == 1 else vmem() for a in ins],
        out_specs=[vmem() for _ in outs],
        cost_estimate=pl.CostEstimate(flops=flops, bytes_accessed=count, transcendentals=0),
        compiler_params=pltpu.CompilerParams(vmem_limit_bytes=limit or 32 * 2**20),
    )(*ins)


def shape(*dims, dtype=BF16):
    return jax.ShapeDtypeStruct(dims, dtype)


def dot(a, b, dims):
    return lax.dot_general(a, b, (dims, ((), ())), preferred_element_type=F32)


def doc_message(key_rows, row_docs):
    tokens, width = key_rows.shape
    plus = row_docs + 1
    row = jnp.concatenate([plus % DOC_BASE, plus // DOC_BASE]).astype(BF16)
    row = jnp.pad(row, (0, width - 2 * tokens))
    return jnp.concatenate([key_rows, jnp.broadcast_to(row[None, :], (LABEL_ROWS, width))], 0)


def column_of(row, eye):
    return jnp.sum(jnp.where(eye, row, 0.0), axis=1, keepdims=True)


def probs_body(q_ref, k_ref, prior_ref, doc_ref, g_ref, pt_ref, back_ref, own_ref):
    tokens = k_ref.shape[0]
    u = lax.broadcasted_iota(jnp.int32, (tokens, tokens), 0)
    t = lax.broadcasted_iota(jnp.int32, (tokens, tokens), 1)
    eye = u == t
    own_docs = doc_ref[...].astype(F32)
    codes = prior_ref[tokens : tokens + LABEL_ROWS, : 2 * tokens].astype(F32)[0:1]
    prior_docs = codes[:, :tokens] + DOC_BASE * codes[:, tokens:] - 1.0
    prior_ok = column_of(prior_docs, eye) == own_docs
    own_ok = (column_of(own_docs, eye) == own_docs) & (u <= t)
    prior_ok = jnp.concatenate([prior_ok] * GROUP, 1)
    own_ok = jnp.concatenate([own_ok] * GROUP, 1)
    scale = 1.0 / math.sqrt(HEAD_DIM)
    for g in range(KV_HEADS):
        heads = [slice((g * GROUP + r) * HEAD_DIM, (g * GROUP + r + 1) * HEAD_DIM) for r in range(GROUP)]
        col = slice(g * HEAD_DIM, (g + 1) * HEAD_DIM)
        q4 = jnp.concatenate([q_ref[:, h] for h in heads], 0)
        g4 = jnp.concatenate([g_ref[:, h] for h in heads], 0)
        sp = jnp.where(prior_ok, dot(prior_ref[:tokens, col], q4, ((1,), (1,))), MASKED)
        so = jnp.where(own_ok, dot(k_ref[:, col], q4, ((1,), (1,))), MASKED)
        top = jnp.maximum(jnp.max(sp, 0, keepdims=True), jnp.max(so, 0, keepdims=True))
        ep = jnp.exp((sp - top) * scale)
        eo = jnp.exp((so - top) * scale)
        inv = 1.0 / (jnp.sum(ep, 0, keepdims=True) + jnp.sum(eo, 0, keepdims=True))
        pp = (ep * inv).astype(BF16)
        po = (eo * inv).astype(BF16)
        pt_ref[g, :tokens, :] = pp
        pt_ref[g, tokens:, :] = po
        back_ref[:, col] = dot(pp, g4, ((1,), (0,))).astype(BF16)
        own_ref[:, col] = dot(po, g4, ((1,), (0,)))


def attend_body(blocks, pt_ref, v_ref, prior_ref, plan_ref, idx_ref, out_ref):
    tokens = v_ref.shape[0]
    rows = tokens // blocks
    owners = out_ref.shape[0]
    data = KV_HEADS * GROUP * rows
    me = idx_ref[0]
    for p in range(owners):
        if owners > blocks:
            out_ref[p, :, :] = jnp.zeros(out_ref.shape[1:], BF16)
    slots = [plan_ref[j] ^ me for j in range(blocks)]
    for j in range(blocks):
        out_ref[slots[j], data:, :] = jnp.full((LABEL_ROWS, LANES), j + 1, F32).astype(BF16)
    for g in range(KV_HEADS):
        col = slice(g * HEAD_DIM, (g + 1) * HEAD_DIM)
        att = dot(pt_ref[g, :tokens, :], prior_ref[:, col], ((0,), (0,)))
        att = (att + dot(pt_ref[g, tokens:, :], v_ref[:, col], ((0,), (0,)))).astype(BF16)
        for r in range(GROUP):
            first = (g * GROUP + r) * rows
            for j in range(blocks):
                at = r * tokens + j * rows
                out_ref[slots[j], first : first + rows, :] = att[at : at + rows]


def place_body(blocks, *refs):
    *arrived, out_ref = refs
    rows = out_ref.shape[0] // blocks
    heads = out_ref.shape[1] // LANES
    for a in arrived:
        label = jnp.max(a[heads * rows : heads * rows + LABEL_ROWS, :].astype(F32)).astype(jnp.int32)

        @pl.when(label > 0)
        def _():
            first = pl.multiple_of((label - 1) * rows, rows)
            for h in range(heads):
                out_ref[pl.ds(first, rows), h * LANES : (h + 1) * LANES] = a[h * rows : (h + 1) * rows, :]


def split_body(owners, chips, idx_ref, in_ref, *outs):
    tokens, width = in_ref.shape
    sub = width // (owners * chips)
    q, z = idx_ref[2], idx_ref[3]
    for k in range(chips):
        for m in range(owners):
            first = pl.multiple_of(((z ^ m) * chips + (q ^ k)) * sub, sub)
            outs[k][m * sub : (m + 1) * sub, :] = in_ref[:, pl.ds(first, sub)].T


def halves_body(idx_ref, own_ref, ret_ref, mine_ref, other_ref):
    half = mine_ref.shape[1]
    c = idx_ref[1]
    for ref, core in ((mine_ref, c), (other_ref, 1 - c)):
        at = pl.ds(pl.multiple_of(core * half, half), half)
        ref[...] = (own_ref[:, at] + ret_ref[:, at].astype(F32)).astype(BF16)


def product_body(owners, chips, *refs):
    a, b, h = refs[:chips], refs[chips : 2 * chips], refs[2 * chips : 3 * chips]
    outs = refs[3 * chips :]
    sub = outs[0].shape[0]
    for m in range(owners):
        rows = slice(m * sub, (m + 1) * sub)
        total = None
        for k in range(chips):
            part = dot(jnp.concatenate([a[k][rows, :], b[k][rows, :]], 1), h[k][...], ((1,), (0,)))
            total = part if total is None else total + part
        outs[m][...] = total.astype(outs[m].dtype)


def sum_body(*refs):
    *terms, out_ref = refs
    total = terms[0][...]
    for term in terms[1:]:
        total = total + term[...].astype(F32)
    out_ref[...] = total.astype(BF16)


def spread_body(chips, idx_ref, *refs):
    mine, other, out_ref = refs[:chips], refs[chips : 2 * chips], refs[2 * chips]
    sub, half = mine[0].shape
    c, q = idx_ref[1], idx_ref[2]
    for k in range(chips):
        rows = pl.ds(pl.multiple_of((q ^ k) * sub, sub), sub)
        for ref, core in ((mine[k], c), (other[k], 1 - c)):
            out_ref[rows, pl.ds(pl.multiple_of(core * half, half), half)] = ref[...].astype(F32)


def weight_by_planes(input_rows, grad_parts, idx):
    owners = lax.axis_size("ctx")
    reps = lax.axis_size("rep")
    plane = ("dp", "rep")
    chips = lax.axis_size(plane) // CORES
    tokens, width = input_rows.shape
    sub = width // (owners * chips)
    masks = [(k // reps) * CORES * reps + k % reps for k in range(chips)]
    pieces = call(
        functools.partial(split_body, owners, chips),
        [shape(owners * sub, tokens)] * chips,
        [idx, input_rows],
    )
    mine_in = [pieces[0]] + [swap(pieces[k], plane, masks[k]) for k in range(1, chips)]
    other_in = [swap(p, "dp", 1) for p in mine_in]
    own_grad, returned = grad_parts()
    kv_width = own_grad.shape[1]
    half = kv_width // CORES
    mine, other = call(halves_body, [shape(tokens, half)] * 2, [idx, own_grad, returned])
    both = jnp.concatenate([mine, swap(other, "dp", 1)], 0)
    grads = [both] + [swap(both, plane, masks[k]) for k in range(1, chips)]
    partial = call(
        functools.partial(product_body, owners, chips),
        [shape(sub, half, dtype=F32)] + [shape(sub, half)] * (owners - 1),
        [*mine_in, *other_in, *grads],
        flops=2 * owners * sub * half * CORES * tokens * chips,
    )
    arrived = [swap(partial[m], "ctx", m) for m in range(1, owners)]
    (total,) = call(sum_body, [shape(sub, half)], [partial[0], *arrived])
    mine_out = [total] + [swap(total, plane, masks[k]) for k in range(1, chips)]
    other_out = [swap(p, "dp", 1) for p in mine_out]
    (result,) = call(
        functools.partial(spread_body, chips),
        [shape(chips * sub, kv_width, dtype=F32)],
        [idx, *mine_out, *other_out],
    )
    return result


def weight_by_collectives(input_rows, grad_parts):
    own_grad, returned = grad_parts()
    grad_values = (own_grad + returned.astype(F32)).astype(BF16)
    term = jnp.einsum("tc,tf->cf", input_rows, grad_values, preferred_element_type=F32).astype(BF16)
    part = lax.psum_scatter(term, "ctx", scatter_dimension=0, tiled=True).astype(F32)
    return lax.psum(part, ("dp", "rep"))


def local(inputs, queries, keys, values, grad_out, doc_ids, plan):
    tokens = inputs.shape[1]
    q_width = queries.shape[2]
    kv_width = keys.shape[2]
    shards = ("ctx", "rep")
    owners = lax.axis_size("dp")
    reps = lax.axis_size("rep")
    blocks = plan.shape[1]
    dp = lax.axis_index("dp")
    idx = jnp.stack(
        [dp, dp % CORES, (dp // CORES) * reps + lax.axis_index("rep"), lax.axis_index("ctx")]
    ).astype(jnp.int32)

    prior_keys = from_behind(doc_message(keys[0], doc_ids[0]), shards, 1)
    prior_values = from_behind(values[0], shards, 1)
    probs, back, own_grad = call(
        probs_body,
        [shape(KV_HEADS, 2 * tokens, GROUP * tokens), shape(tokens, kv_width), shape(tokens, kv_width, dtype=F32)],
        [queries[0], keys[0], prior_keys, doc_ids, grad_out[0]],
        flops=8 * tokens * tokens * q_width,
    )

    rows = tokens // blocks
    (outgoing,) = call(
        functools.partial(attend_body, blocks),
        [shape(owners, (q_width // LANES) * rows + LABEL_ROWS, LANES)],
        [probs, values[0], prior_values, plan[0], idx],
        flops=4 * tokens * tokens * q_width,
    )
    arrived = [outgoing[0]] + [swap(outgoing[m], "dp", m) for m in range(1, owners)]
    (placed,) = call(functools.partial(place_body, blocks), [shape(tokens, q_width)], arrived)

    def grad_parts():
        return own_grad, from_behind(back, shards, -1)

    sub = inputs.shape[2] // (lax.axis_size("ctx") * owners // CORES * reps)
    if sub % LANES == 0:
        weight_grad = weight_by_planes(inputs[0], grad_parts, idx)
    else:
        weight_grad = weight_by_collectives(inputs[0], grad_parts)
    return (placed[None], weight_grad)


def solution(mesh):
    rows = P("dp", ("ctx", "rep"), None)
    ids = P("dp", ("ctx", "rep"))
    return jax.shard_map(
        local,
        mesh=mesh,
        in_specs=(rows, rows, rows, rows, rows, ids, ids),
        out_specs=(rows, P("ctx", None)),
        check_vma=False,
    )
```

```python
import functools
import math

import jax
import jax.numpy as jnp
from jax import lax
from jax.experimental import pallas as pl
from jax.experimental.pallas import tpu as pltpu
from jax.sharding import PartitionSpec as P

HEAD_DIM = 128
KV_HEADS = 4
GROUP = 4
CORES = 2
LANES = 128
LABEL_ROWS = 16
DOC_BASE = 128
MASKED = -1e30
BF16 = jnp.bfloat16
F32 = jnp.float32


def from_behind(value, axis, by):
    devices = lax.axis_size(axis)
    pairs = [(i, i + by) for i in range(devices) if 0 <= i + by < devices]
    return lax.ppermute(value, axis, pairs)


def swap(value, axis, mask):
    devices = lax.axis_size(axis)
    return lax.ppermute(value, axis, [(i, i ^ mask) for i in range(devices)])


def vmem():
    return pl.BlockSpec(memory_space=pltpu.VMEM)


def smem():
    return pl.BlockSpec(memory_space=pltpu.SMEM)


def call(body, outs, ins, weight=0, deps=(), hbm_in=(), hbm_out=(), scratch=()):
    space = pl.BlockSpec(memory_space=pltpu.HBM)
    ins_at = [smem() if a.dtype == jnp.int32 and a.ndim == 1 else vmem() for a in ins]
    ins_at = [space if i in hbm_in else at for i, at in enumerate(ins_at)]
    skip = len(deps)
    ins = [pltpu.with_memory_space_constraint(a, pltpu.HBM) if i in hbm_in else a for i, a in enumerate(ins)]
    return pl.pallas_call(
        lambda *refs: body(*refs[skip:]),
        out_shape=outs,
        in_specs=[space] * skip + ins_at,
        out_specs=[space if i in hbm_out else vmem() for i in range(len(outs))],
        scratch_shapes=list(scratch),
        cost_estimate=pl.CostEstimate(flops=weight * 10**9, bytes_accessed=0, transcendentals=0),
        compiler_params=pltpu.CompilerParams(vmem_limit_bytes=32 * 2**20),
    )(*deps, *ins)


def shape(*dims, dtype=BF16):
    return jax.ShapeDtypeStruct(dims, dtype)


def dot(a, b, dims):
    return lax.dot_general(a, b, (dims, ((), ())), preferred_element_type=F32)


def message_body(key_hbm, value_hbm, doc_hbm, out_ref, doc_ref, sems):
    tokens, width = key_hbm.shape
    copies = [
        pltpu.make_async_copy(ref, out_ref.at[pl.ds(i * tokens, tokens)], sems.at[i])
        for i, ref in enumerate((key_hbm, value_hbm))
    ]
    copies.append(pltpu.make_async_copy(doc_hbm, doc_ref, sems.at[2]))
    for copy in copies:
        copy.start()
    copies.pop().wait()
    plus = doc_ref[...] + 1
    high = plus // DOC_BASE
    digits = jnp.concatenate([plus - high * DOC_BASE, high], 1).astype(F32)
    digits = jnp.broadcast_to(digits, (LABEL_ROWS, 2 * tokens)).astype(BF16)
    out_ref[2 * tokens :, : 2 * tokens] = digits
    if width > 2 * tokens:
        out_ref[2 * tokens :, 2 * tokens :] = jnp.zeros((LABEL_ROWS, width - 2 * tokens), BF16)
    for copy in copies:
        copy.wait()


def docs_of(message_ref, tokens):
    codes = message_ref[2 * tokens :, : 2 * tokens].astype(F32)[0:1]
    return codes[:, :tokens] + DOC_BASE * codes[:, tokens:] - 1.0


def column_of(row, eye):
    return jnp.sum(jnp.where(eye, row, 0.0), axis=1, keepdims=True)


def probs_body(q_ref, g_ref, k_ref, prior_ref, pt_ref, back_ref, own_ref):
    tokens = q_ref.shape[0]
    u = lax.broadcasted_iota(jnp.int32, (tokens, tokens), 0)
    t = lax.broadcasted_iota(jnp.int32, (tokens, tokens), 1)
    eye = u == t
    own_docs = docs_of(k_ref, tokens)
    prior_ok = column_of(docs_of(prior_ref, tokens), eye) == own_docs
    own_ok = (column_of(own_docs, eye) == own_docs) & (u <= t)
    prior_ok = jnp.concatenate([prior_ok] * GROUP, 1)
    own_ok = jnp.concatenate([own_ok] * GROUP, 1)
    scale = 1.0 / math.sqrt(HEAD_DIM)
    for g in range(KV_HEADS):
        heads = [slice((g * GROUP + r) * HEAD_DIM, (g * GROUP + r + 1) * HEAD_DIM) for r in range(GROUP)]
        col = slice(g * HEAD_DIM, (g + 1) * HEAD_DIM)
        q4 = jnp.concatenate([q_ref[:, h] for h in heads], 0)
        g4 = jnp.concatenate([g_ref[:, h] for h in heads], 0)
        sp = jnp.where(prior_ok, dot(prior_ref[:tokens, col], q4, ((1,), (1,))), MASKED)
        so = jnp.where(own_ok, dot(k_ref[:tokens, col], q4, ((1,), (1,))), MASKED)
        top = jnp.maximum(jnp.max(sp, 0, keepdims=True), jnp.max(so, 0, keepdims=True))
        ep = jnp.exp((sp - top) * scale)
        eo = jnp.exp((so - top) * scale)
        inv = 1.0 / (jnp.sum(ep, 0, keepdims=True) + jnp.sum(eo, 0, keepdims=True))
        pp = (ep * inv).astype(BF16)
        po = (eo * inv).astype(BF16)
        pt_ref[g, :tokens, :] = pp
        pt_ref[g, tokens:, :] = po
        back_ref[:, col] = dot(pp, g4, ((1,), (0,))).astype(BF16)
        own_ref[:, col] = dot(po, g4, ((1,), (0,)))


def attend_body(blocks, pt_ref, message_ref, prior_ref, plan_ref, idx_ref, out_ref):
    tokens = pt_ref.shape[1] // 2
    rows = tokens // blocks
    owners = out_ref.shape[0]
    data = KV_HEADS * GROUP * rows
    me = idx_ref[0]
    if owners > blocks:
        out_ref[...] = jnp.zeros(out_ref.shape, BF16)
    slots = [plan_ref[j] ^ me for j in range(blocks)]
    for j in range(blocks):
        out_ref[slots[j], data:, :] = jnp.full((LABEL_ROWS, LANES), j + 1, F32).astype(BF16)
    for g in range(KV_HEADS):
        col = slice(g * HEAD_DIM, (g + 1) * HEAD_DIM)
        att = dot(pt_ref[g, :tokens, :], prior_ref[tokens : 2 * tokens, col], ((0,), (0,)))
        att = att + dot(pt_ref[g, tokens:, :], message_ref[tokens : 2 * tokens, col], ((0,), (0,)))
        att = att.astype(BF16)
        for r in range(GROUP):
            first = (g * GROUP + r) * rows
            for j in range(blocks):
                at = r * tokens + j * rows
                out_ref[slots[j], first : first + rows, :] = att[at : at + rows]


def place_body(blocks, *refs):
    *arrived, out_hbm, wide_ref, sems = refs
    rows = out_hbm.shape[0] // blocks
    heads = out_hbm.shape[1] // LANES
    labels = [jnp.max(a[heads * rows :, :].astype(F32)).astype(jnp.int32) for a in arrived]
    copies = []
    for i, a in enumerate(arrived):
        first = pl.multiple_of(jnp.maximum(labels[i] - 1, 0) * rows, rows)
        copies.append(pltpu.make_async_copy(wide_ref.at[i], out_hbm.at[pl.ds(first, rows)], sems.at[i]))

        @pl.when(labels[i] > 0)
        def _():
            for h in range(heads):
                wide_ref[i, :, h * LANES : (h + 1) * LANES] = a[h * rows : (h + 1) * rows, :]
            copies[i].start()

    for i, copy in enumerate(copies):

        @pl.when(labels[i] > 0)
        def _():
            copy.wait()


def split_body(reduced, places, idx_ref, in_hbm, q_hbm, g_hbm, *refs):
    spread = len(places)
    outs, (q_ref, g_ref, in_ref, sems) = refs[:spread], refs[spread:]
    copies = [
        pltpu.make_async_copy(src, dst, sems.at[i])
        for i, (src, dst) in enumerate(((in_hbm, in_ref), (q_hbm, q_ref), (g_hbm, g_ref)))
    ]
    for copy in copies:
        copy.start()
    sub = in_ref.shape[1] // (spread * len(reduced))
    x, y, z = idx_ref[2], idx_ref[3], idx_ref[4]
    reps, chips = idx_ref[5], idx_ref[6]
    copies[0].wait()
    for k, (kx, kz, ky) in enumerate(places):
        for m, (mx, mz, my) in enumerate(reduced):
            first = (z ^ kz ^ mz) * chips + (x ^ kx ^ mx) * reps + (y ^ ky ^ my)
            first = pl.multiple_of(first * sub, sub)
            outs[k][m * sub : (m + 1) * sub, :] = in_ref[:, pl.ds(first, sub)].T
    copies[1].wait()
    copies[2].wait()


def both_body(own_ref, ret_ref, out_ref):
    out_ref[...] = (own_ref[...] + ret_ref[...].astype(F32)).astype(BF16)


def product_body(cross, idx_ref, *refs):
    *ins, out_ref = refs
    count = len(ins) // 2
    half = out_ref.shape[1]
    core = idx_ref[1] ^ 1 if cross else idx_ref[1]
    cols = pl.ds(pl.multiple_of(core * half, half), half)
    a = jnp.concatenate([ref[...] for ref in ins[:count]], 1)
    b = jnp.concatenate([ref[:, cols] for ref in ins[count:]], 0)
    out_ref[...] = dot(a, b, ((1,), (0,))).astype(out_ref.dtype)


def add_body(own_ref, cross_ref, *outs):
    sub = outs[0].shape[0]
    for m, out in enumerate(outs):
        rows = slice(m * sub, (m + 1) * sub)
        out[...] = (own_ref[rows, :] + cross_ref[rows, :].astype(F32)).astype(out.dtype)


def sum_body(*refs):
    *terms, out_ref = refs
    total = terms[0][...]
    for term in terms[1:]:
        total = total + term[...].astype(F32)
    out_ref[...] = total.astype(BF16)


def spread_body(chips, idx_ref, *refs):
    mine, other, (out_hbm, wide_ref, sems) = refs[:chips], refs[chips : 2 * chips], refs[2 * chips :]
    sub, half = mine[0].shape
    c, q = idx_ref[1], idx_ref[2] * idx_ref[5] + idx_ref[3]
    copies = []
    for k in range(chips):
        rows = pl.ds(pl.multiple_of((q ^ k) * sub, sub), sub)
        for i, (ref, core) in enumerate(((mine[k], c), (other[k], 1 - c))):
            at = 2 * k + i
            wide_ref[at] = ref[...].astype(F32)
            to = out_hbm.at[rows, pl.ds(pl.multiple_of(core * half, half), half)]
            copies.append(pltpu.make_async_copy(wide_ref.at[at], to, sems.at[at]))
            copies[-1].start()
    for copy in copies:
        copy.wait()


def weight_by_collectives(input_rows, grad_parts):
    own_grad, returned = grad_parts()
    grad_values = (own_grad + returned.astype(F32)).astype(BF16)
    term = jnp.einsum("tc,tf->cf", input_rows, grad_values, preferred_element_type=F32).astype(BF16)
    part = lax.psum_scatter(term, "ctx", scatter_dimension=0, tiled=True).astype(F32)
    return lax.psum(part, ("dp", "rep"))


def weight_by_collectives(input_rows, own_grad, returned):
    grad_values = (own_grad + returned.astype(F32)).astype(BF16)
    term = jnp.einsum("tc,tf->cf", input_rows, grad_values, preferred_element_type=F32).astype(BF16)
    part = lax.psum_scatter(term, "ctx", scatter_dimension=0, tiled=True).astype(F32)
    return lax.psum(part, ("dp", "rep"))


def local(inputs, queries, keys, values, grad_out, doc_ids, plan):
    tokens, width = inputs.shape[1:]
    q_width = queries.shape[2]
    kv_width = keys.shape[2]
    half = kv_width // CORES
    shards = ("ctx", "rep")
    micro, owners, reps = (lax.axis_size(axis) for axis in ("dp", "ctx", "rep"))
    chips = micro // CORES * reps
    blocks = plan.shape[1]
    rows = tokens // blocks
    dp, ctx, rep = (lax.axis_index(axis) for axis in ("dp", "ctx", "rep"))
    idx = jnp.stack([dp, dp % CORES, dp // CORES, rep, ctx, reps, chips]).astype(jnp.int32)

    places = [(kx, 0, ky) for kx in range(micro // CORES) for ky in range(reps)]
    reduced = [(0, mz, 0) for mz in range(owners)]
    every = ("dp", "ctx", "rep")

    def away(value, x, z, y):
        return swap(value, every, (x * CORES * owners + z) * reps + y)

    sub = width // (len(places) * len(reduced))
    by_chips = sub % LANES == 0

    (message,) = call(
        message_body,
        [shape(2 * tokens + LABEL_ROWS, kv_width)],
        [keys[0], values[0], doc_ids],
        hbm_in=(0, 1, 2),
        scratch=[pltpu.VMEM(doc_ids.shape, jnp.int32), pltpu.SemaphoreType.DMA((3,))],
    )
    prior = from_behind(message, shards, 1)

    if by_chips:
        *pieces, q_rows, g_rows = call(
            functools.partial(split_body, reduced, places),
            [shape(len(reduced) * sub, tokens)] * len(places) + [shape(tokens, q_width)] * 2,
            [idx, inputs[0], queries[0], grad_out[0]],
            hbm_in=(1, 2, 3),
            scratch=[pltpu.VMEM((tokens, width), BF16), pltpu.SemaphoreType.DMA((3,))],
        )

        def gather(value_of):
            return [value_of(0)] + [away(value_of(k), *place) for k, place in enumerate(places) if k]

        mine_in = gather(lambda k: pieces[k])
    else:
        q_rows, g_rows = queries[0], grad_out[0]

    probs, back, own = call(
        probs_body,
        [
            shape(KV_HEADS, 2 * tokens, GROUP * tokens),
            shape(tokens, kv_width),
            shape(tokens, kv_width, dtype=F32),
        ],
        [q_rows, g_rows, message, prior],
        weight=100,
    )
    returned = from_behind(back, shards, -1)
    if by_chips:
        (grad_values,) = call(both_body, [shape(tokens, kv_width)], [own, returned])
        grads = gather(lambda k: grad_values)
        factors = [idx, *mine_in, *grads]
        (cross,) = call(functools.partial(product_body, True), [shape(len(reduced) * sub, half)], factors)
        (kept,) = call(
            functools.partial(product_body, False), [shape(len(reduced) * sub, half, dtype=F32)], factors, weight=3
        )
        partial = call(
            add_body,
            [shape(sub, half, dtype=F32)] + [shape(sub, half)] * (len(reduced) - 1),
            [kept, swap(cross, "dp", 1)],
        )
        arrived = [away(partial[m], *place) for m, place in enumerate(reduced) if m]

    (outgoing,) = call(
        functools.partial(attend_body, blocks),
        [shape(micro, (q_width // LANES) * rows + LABEL_ROWS, LANES)],
        [probs, message, prior, plan[0], idx],
        weight=100,
        deps=[partial[0]] if by_chips else [],
    )
    arrived_out = [outgoing[0]] + [swap(outgoing[m], "dp", m) for m in range(1, micro)]

    (placed,) = call(
        functools.partial(place_body, blocks),
        [shape(tokens, q_width)],
        arrived_out,
        hbm_out=(0,),
        scratch=[pltpu.VMEM((micro, rows, q_width), BF16), pltpu.SemaphoreType.DMA((micro,))],
    )
    if by_chips:
        (total,) = call(sum_body, [shape(sub, half)], [partial[0], *arrived], deps=[outgoing])
        mine_out = [total] + [away(total, k // reps, 0, k % reps) for k in range(1, chips)]
        other_out = [swap(p, "dp", 1) for p in mine_out]
        (weight_grad,) = call(
            functools.partial(spread_body, chips),
            [shape(chips * sub, kv_width, dtype=F32)],
            [idx, *mine_out, *other_out],
            hbm_out=(0,),
            scratch=[pltpu.VMEM((2 * chips, sub, half), F32), pltpu.SemaphoreType.DMA((2 * chips,))],
        )
    else:
        weight_grad = weight_by_collectives(inputs[0], own, returned)
    return (placed[None], weight_grad)


def solution(mesh):
    rows = P("dp", ("ctx", "rep"), None)
    ids = P("dp", ("ctx", "rep"))
    return jax.shard_map(
        local,
        mesh=mesh,
        in_specs=(rows, rows, rows, rows, rows, ids, ids),
        out_specs=(rows, P("ctx", None)),
        check_vma=False,
    )
```

```python
import functools
import math

import jax
import jax.numpy as jnp
from jax import lax
from jax.experimental import pallas as pl
from jax.experimental.pallas import tpu as pltpu
from jax.sharding import PartitionSpec as P

HEAD_DIM = 128
KV_HEADS = 4
GROUP = 4
CORES = 2
LANES = 128
LABEL_ROWS = 16
DOC_BASE = 128
MASKED = -1e30
BF16 = jnp.bfloat16
F32 = jnp.float32


def from_behind(value, axis, by):
    devices = lax.axis_size(axis)
    pairs = [(i, i + by) for i in range(devices) if 0 <= i + by < devices]
    return lax.ppermute(value, axis, pairs)


def swap(value, axis, mask):
    devices = lax.axis_size(axis)
    return lax.ppermute(value, axis, [(i, i ^ mask) for i in range(devices)])


def chip_at():
    dp = lax.axis_index("dp")
    return dp % CORES, dp // CORES, lax.axis_index("ctx"), lax.axis_index("rep")


def vmem():
    return pl.BlockSpec(memory_space=pltpu.VMEM)


def smem():
    return pl.BlockSpec(memory_space=pltpu.SMEM)


def call(body, outs, ins, weight=0, deps=(), hbm_in=(), hbm_out=(), scratch=(), alias={}):
    space = pl.BlockSpec(memory_space=pltpu.HBM)
    ins_at = [smem() if a.dtype == jnp.int32 and a.ndim == 1 else vmem() for a in ins]
    ins_at = [space if i in hbm_in else at for i, at in enumerate(ins_at)]
    skip = len(deps)
    ins = [pltpu.with_memory_space_constraint(a, pltpu.HBM) if i in hbm_in else a for i, a in enumerate(ins)]
    return pl.pallas_call(
        lambda *refs: body(*refs[skip:]),
        out_shape=[pltpu.HBM(o.shape, o.dtype) if i in hbm_out else o for i, o in enumerate(outs)],
        in_specs=[space] * skip + ins_at,
        out_specs=[space if i in hbm_out else vmem() for i in range(len(outs))],
        scratch_shapes=list(scratch),
        input_output_aliases={skip + i: o for i, o in alias.items()},
        cost_estimate=pl.CostEstimate(flops=weight * 10**9, bytes_accessed=0, transcendentals=0),
        compiler_params=pltpu.CompilerParams(vmem_limit_bytes=32 * 2**20),
    )(*deps, *ins)


def shape(*dims, dtype=BF16):
    return jax.ShapeDtypeStruct(dims, dtype)


def dot(a, b, dims):
    return lax.dot_general(a, b, (dims, ((), ())), preferred_element_type=F32)


def message_body(key_hbm, value_hbm, doc_hbm, out_ref, doc_ref, sems):
    tokens, width = key_hbm.shape
    copies = [
        pltpu.make_async_copy(ref, out_ref.at[pl.ds(i * tokens, tokens)], sems.at[i])
        for i, ref in enumerate((key_hbm, value_hbm))
    ]
    copies.append(pltpu.make_async_copy(doc_hbm, doc_ref, sems.at[2]))
    for copy in copies:
        copy.start()
    copies.pop().wait()
    plus = doc_ref[...] + 1
    high = plus // DOC_BASE
    digits = jnp.concatenate([plus - high * DOC_BASE, high], 1).astype(F32)
    digits = jnp.broadcast_to(digits, (LABEL_ROWS, 2 * tokens)).astype(BF16)
    out_ref[2 * tokens :, : 2 * tokens] = digits
    if width > 2 * tokens:
        out_ref[2 * tokens :, 2 * tokens :] = jnp.zeros((LABEL_ROWS, width - 2 * tokens), BF16)
    for copy in copies:
        copy.wait()


def docs_of(message_ref, tokens):
    codes = message_ref[2 * tokens :, : 2 * tokens].astype(F32)[0:1]
    return codes[:, :tokens] + DOC_BASE * codes[:, tokens:] - 1.0


def column_of(row, eye):
    return jnp.sum(jnp.where(eye, row, 0.0), axis=1, keepdims=True)


def probs_body(q_ref, g_ref, k_ref, prior_ref, pt_ref, back_ref, own_ref):
    tokens = q_ref.shape[0]
    u = lax.broadcasted_iota(jnp.int32, (tokens, tokens), 0)
    t = lax.broadcasted_iota(jnp.int32, (tokens, tokens), 1)
    eye = u == t
    own_docs = docs_of(k_ref, tokens)
    prior_ok = column_of(docs_of(prior_ref, tokens), eye) == own_docs
    own_ok = (column_of(own_docs, eye) == own_docs) & (u <= t)
    prior_ok = jnp.concatenate([prior_ok] * GROUP, 1)
    own_ok = jnp.concatenate([own_ok] * GROUP, 1)
    scale = 1.0 / math.sqrt(HEAD_DIM)
    for g in range(KV_HEADS):
        heads = [slice((g * GROUP + r) * HEAD_DIM, (g * GROUP + r + 1) * HEAD_DIM) for r in range(GROUP)]
        col = slice(g * HEAD_DIM, (g + 1) * HEAD_DIM)
        q4 = jnp.concatenate([q_ref[:, h] for h in heads], 0)
        g4 = jnp.concatenate([g_ref[:, h] for h in heads], 0)
        sp = jnp.where(prior_ok, dot(prior_ref[:tokens, col], q4, ((1,), (1,))), MASKED)
        so = jnp.where(own_ok, dot(k_ref[:tokens, col], q4, ((1,), (1,))), MASKED)
        top = jnp.maximum(jnp.max(sp, 0, keepdims=True), jnp.max(so, 0, keepdims=True))
        ep = jnp.exp((sp - top) * scale)
        eo = jnp.exp((so - top) * scale)
        inv = 1.0 / (jnp.sum(ep, 0, keepdims=True) + jnp.sum(eo, 0, keepdims=True))
        pp = (ep * inv).astype(BF16)
        po = (eo * inv).astype(BF16)
        pt_ref[g, :tokens, :] = pp
        pt_ref[g, tokens:, :] = po
        back_ref[:, col] = dot(pp, g4, ((1,), (0,))).astype(BF16)
        own_ref[:, col] = dot(po, g4, ((1,), (0,)))


def attend_body(blocks, pt_ref, message_ref, prior_ref, plan_ref, out_ref):
    tokens = pt_ref.shape[1] // 2
    rows = tokens // blocks
    owners = out_ref.shape[0]
    data = KV_HEADS * GROUP * rows
    me = lax.axis_index("dp")
    if owners > blocks:
        out_ref[...] = jnp.zeros(out_ref.shape, BF16)
    slots = [plan_ref[j] ^ me for j in range(blocks)]
    for j in range(blocks):
        out_ref[slots[j], data:, :] = jnp.full((LABEL_ROWS, LANES), j + 1, F32).astype(BF16)
    for g in range(KV_HEADS):
        col = slice(g * HEAD_DIM, (g + 1) * HEAD_DIM)
        att = dot(pt_ref[g, :tokens, :], prior_ref[tokens : 2 * tokens, col], ((0,), (0,)))
        att = att + dot(pt_ref[g, tokens:, :], message_ref[tokens : 2 * tokens, col], ((0,), (0,)))
        att = att.astype(BF16)
        for r in range(GROUP):
            first = (g * GROUP + r) * rows
            for j in range(blocks):
                at = r * tokens + j * rows
                out_ref[slots[j], first : first + rows, :] = att[at : at + rows]


def place_body(blocks, *refs):
    *arrived, out_hbm, wide_ref, sems = refs
    rows = out_hbm.shape[0] // blocks
    heads = out_hbm.shape[1] // LANES
    labels = [jnp.max(a[heads * rows :, :].astype(F32)).astype(jnp.int32) for a in arrived]
    copies = []
    for i, a in enumerate(arrived):
        first = pl.multiple_of(jnp.maximum(labels[i] - 1, 0) * rows, rows)
        copies.append(pltpu.make_async_copy(wide_ref.at[i], out_hbm.at[pl.ds(first, rows)], sems.at[i]))

        @pl.when(labels[i] > 0)
        def _():
            for h in range(heads):
                wide_ref[i, :, h * LANES : (h + 1) * LANES] = a[h * rows : (h + 1) * rows, :]
            copies[i].start()

    for i, copy in enumerate(copies):

        @pl.when(labels[i] > 0)
        def _():
            copy.wait()


def split_body(reduced, places, chips, in_hbm, q_hbm, g_hbm, *refs):
    spread = len(places)
    outs, (q_ref, g_ref, in_ref, sems) = refs[:spread], refs[spread:]
    copies = [
        pltpu.make_async_copy(src, dst, sems.at[i])
        for i, (src, dst) in enumerate(((in_hbm, in_ref), (q_hbm, q_ref), (g_hbm, g_ref)))
    ]
    for copy in copies:
        copy.start()
    sub = in_ref.shape[1] // (spread * len(reduced))
    core, x, z, y = chip_at()
    reps = lax.axis_size("rep")
    copies[0].wait()
    for k, (kx, kz, ky) in enumerate(places):
        for m, (mx, mz, my) in enumerate(reduced):
            first = (z ^ kz ^ mz) * chips + (x ^ kx ^ mx) * reps + (y ^ ky ^ my)
            first = pl.multiple_of(first * sub, sub)
            outs[k][m * sub : (m + 1) * sub, :] = in_ref[:, pl.ds(first, sub)].T
    copies[1].wait()
    copies[2].wait()


def both_body(own_ref, ret_ref, out_ref):
    out_ref[...] = (own_ref[...] + ret_ref[...].astype(F32)).astype(BF16)


def product_body(cross, *refs):
    *ins, out_ref = refs
    count = len(ins) // 2
    half = out_ref.shape[1]
    core = chip_at()[0] ^ cross
    cols = pl.ds(pl.multiple_of(core * half, half), half)
    a = jnp.concatenate([ref[...] for ref in ins[:count]], 1)
    b = jnp.concatenate([ref[:, cols] for ref in ins[count:]], 0)
    out_ref[...] = dot(a, b, ((1,), (0,))).astype(out_ref.dtype)


def add_body(own_ref, cross_ref, *outs):
    sub = outs[0].shape[0]
    for m, out in enumerate(outs):
        rows = slice(m * sub, (m + 1) * sub)
        out[...] = (own_ref[rows, :] + cross_ref[rows, :].astype(F32)).astype(out.dtype)


def sum_body(*refs):
    *terms, out_ref = refs
    total = terms[0][...]
    for term in terms[1:]:
        total = total + term[...].astype(F32)
    out_ref[...] = total.astype(BF16)


def spread_body(blocks, *refs):
    pieces = refs[: len(blocks)]
    out_hbm, wide_ref, sems = refs[-3:]
    sub, half = pieces[0].shape
    core, x, _, y = chip_at()
    q = x * lax.axis_size("rep") + y
    copies = []
    for i, (k, other) in enumerate(blocks):
        wide_ref[i] = pieces[i][...].astype(F32)
        rows = pl.ds(pl.multiple_of((q ^ k) * sub, sub), sub)
        cols = pl.ds(pl.multiple_of((core ^ other) * half, half), half)
        copies.append(pltpu.make_async_copy(wide_ref.at[i], out_hbm.at[rows, cols], sems.at[i]))
        copies[i].start()
    for copy in copies:
        copy.wait()


def weight_by_collectives(input_rows, grad_parts):
    own_grad, returned = grad_parts()
    grad_values = (own_grad + returned.astype(F32)).astype(BF16)
    term = jnp.einsum("tc,tf->cf", input_rows, grad_values, preferred_element_type=F32).astype(BF16)
    part = lax.psum_scatter(term, "ctx", scatter_dimension=0, tiled=True).astype(F32)
    return lax.psum(part, ("dp", "rep"))


def weight_by_collectives(input_rows, own_grad, returned):
    grad_values = (own_grad + returned.astype(F32)).astype(BF16)
    term = jnp.einsum("tc,tf->cf", input_rows, grad_values, preferred_element_type=F32).astype(BF16)
    part = lax.psum_scatter(term, "ctx", scatter_dimension=0, tiled=True).astype(F32)
    return lax.psum(part, ("dp", "rep"))


def local(inputs, queries, keys, values, grad_out, doc_ids, plan):
    tokens, width = inputs.shape[1:]
    q_width = queries.shape[2]
    kv_width = keys.shape[2]
    half = kv_width // CORES
    shards = ("ctx", "rep")
    micro, owners, reps = (lax.axis_size(axis) for axis in ("dp", "ctx", "rep"))
    chips = micro // CORES * reps
    blocks = plan.shape[1]
    rows = tokens // blocks

    places = [(kx, kz, 0) for kx in range(micro // CORES) for kz in range(2)]
    reduced = [(0, 2 * mz, my) for mz in range(owners // 2) for my in range(reps)]
    every = ("dp", "ctx", "rep")

    def away(value, x, z, y):
        return swap(value, every, (x * CORES * owners + z) * reps + y)

    sub = width // (len(places) * len(reduced))
    by_chips = sub % LANES == 0

    (message,) = call(
        message_body,
        [shape(2 * tokens + LABEL_ROWS, kv_width)],
        [keys[0], values[0], doc_ids],
        hbm_in=(0, 1, 2),
        scratch=[pltpu.VMEM(doc_ids.shape, jnp.int32), pltpu.SemaphoreType.DMA((3,))],
    )
    prior = from_behind(message, shards, 1)

    if by_chips:
        *pieces, q_rows, g_rows = call(
            functools.partial(split_body, reduced, places, chips),
            [shape(len(reduced) * sub, tokens)] * len(places) + [shape(tokens, q_width)] * 2,
            [inputs[0], queries[0], grad_out[0]],
            hbm_in=(0, 1, 2),
            scratch=[pltpu.VMEM((tokens, width), BF16), pltpu.SemaphoreType.DMA((3,))],
        )

        def gather(value_of):
            far_first = [away(value_of(k), *place) for k, place in reversed([*enumerate(places)]) if k]
            return far_first + [value_of(0)]

        mine_in = gather(lambda k: pieces[k])
    else:
        q_rows, g_rows = queries[0], grad_out[0]

    probs, back, own = call(
        probs_body,
        [
            shape(KV_HEADS, 2 * tokens, GROUP * tokens),
            shape(tokens, kv_width),
            shape(tokens, kv_width, dtype=F32),
        ],
        [q_rows, g_rows, message, prior],
        weight=100,
    )
    returned = from_behind(back, shards, -1)
    if by_chips:
        (grad_values,) = call(both_body, [shape(tokens, kv_width)], [own, returned], deps=mine_in[1:3])
        grads = gather(lambda k: grad_values)
        factors = [*mine_in, *grads]
        (cross,) = call(functools.partial(product_body, 1), [shape(len(reduced) * sub, half)], factors)
        (kept,) = call(
            functools.partial(product_body, 0), [shape(len(reduced) * sub, half, dtype=F32)], factors, weight=3
        )
        partial = call(
            add_body,
            [shape(sub, half, dtype=F32)] + [shape(sub, half)] * (len(reduced) - 1),
            [kept, swap(cross, "dp", 1)],
        )
        arrived = [away(partial[m], *reduced[m]) for m in (*range(2, len(reduced)), 1)]

    (outgoing,) = call(
        functools.partial(attend_body, blocks),
        [shape(micro, (q_width // LANES) * rows + LABEL_ROWS, LANES)],
        [probs, message, prior, plan[0]],
        weight=100,
        deps=[partial[0]] if by_chips else [],
    )
    arrived_out = [outgoing[0]] + [swap(outgoing[m], "dp", m) for m in range(1, micro)]

    (placed,) = call(
        functools.partial(place_body, blocks),
        [shape(tokens, q_width)],
        arrived_out,
        hbm_out=(0,),
        scratch=[pltpu.VMEM((micro, rows, q_width), BF16), pltpu.SemaphoreType.DMA((micro,))],
        weight=2,
    )
    if by_chips:
        (total,) = call(sum_body, [shape(sub, half)], [partial[0], *arrived], deps=[outgoing])
        last = chips - 1
        sums = [away(total, k // reps, 0, k % reps) for k in reversed(range(1, chips))]
        sums = [total, *reversed(sums)]
        others = [swap(p, "dp", 1) for p in sums]

        def spread(chosen, so_far=(), weight=0):
            blocks = [(k, other) for k in chosen for other in range(CORES)]
            pieces = [(others if other else sums)[k] for k, other in blocks]
            (result,) = call(
                functools.partial(spread_body, blocks),
                [shape(chips * sub, kv_width, dtype=F32)],
                [*pieces, *so_far],
                weight=weight,
                hbm_in=(len(pieces),),
                hbm_out=(0,),
                scratch=[pltpu.VMEM((len(blocks), sub, half), F32), pltpu.SemaphoreType.DMA((len(blocks),))],
                alias={len(pieces): 0} if so_far else {},
            )
            return result

        weight_grad = spread([last], [spread(range(last), weight=2)])
    else:
        weight_grad = weight_by_collectives(inputs[0], own, returned)
    return (placed[None], weight_grad)


def solution(mesh):
    rows = P("dp", ("ctx", "rep"), None)
    ids = P("dp", ("ctx", "rep"))
    return jax.shard_map(
        local,
        mesh=mesh,
        in_specs=(rows, rows, rows, rows, rows, ids, ids),
        out_specs=(rows, P("ctx", None)),
        check_vma=False,
    )
```

```python
import functools
import math

import jax
import jax.numpy as jnp
from jax import lax
from jax.experimental import pallas as pl
from jax.experimental.pallas import tpu as pltpu
from jax.sharding import PartitionSpec as P

HEAD_DIM = 128
KV_HEADS = 4
GROUP = 4
CORES = 2
LANES = 128
LABEL_ROWS = 16
DOC_BASE = 128
MASKED = -1e30
BF16 = jnp.bfloat16
F32 = jnp.float32


def from_behind(value, axis, by):
    devices = lax.axis_size(axis)
    pairs = [(i, i + by) for i in range(devices) if 0 <= i + by < devices]
    return lax.ppermute(value, axis, pairs)


def swap(value, axis, mask):
    devices = lax.axis_size(axis)
    return lax.ppermute(value, axis, [(i, i ^ mask) for i in range(devices)])


def chip_at():
    dp = lax.axis_index("dp")
    return dp % CORES, dp // CORES, lax.axis_index("ctx"), lax.axis_index("rep")


def vmem():
    return pl.BlockSpec(memory_space=pltpu.VMEM)


def smem():
    return pl.BlockSpec(memory_space=pltpu.SMEM)


def call(body, outs, ins, weight=0, deps=(), hbm_in=(), hbm_out=(), scratch=(), alias={}):
    space = pl.BlockSpec(memory_space=pltpu.HBM)
    ins_at = [smem() if a.dtype == jnp.int32 and a.ndim == 1 else vmem() for a in ins]
    ins_at = [space if i in hbm_in else at for i, at in enumerate(ins_at)]
    skip = len(deps)
    ins = [pltpu.with_memory_space_constraint(a, pltpu.HBM) if i in hbm_in else a for i, a in enumerate(ins)]
    return pl.pallas_call(
        lambda *refs: body(*refs[skip:]),
        out_shape=[pltpu.HBM(o.shape, o.dtype) if i in hbm_out else o for i, o in enumerate(outs)],
        in_specs=[space] * skip + ins_at,
        out_specs=[space if i in hbm_out else vmem() for i in range(len(outs))],
        scratch_shapes=list(scratch),
        input_output_aliases={skip + i: o for i, o in alias.items()},
        cost_estimate=pl.CostEstimate(flops=weight * 10**9, bytes_accessed=0, transcendentals=0),
        compiler_params=pltpu.CompilerParams(vmem_limit_bytes=32 * 2**20),
    )(*deps, *ins)


def shape(*dims, dtype=BF16):
    return jax.ShapeDtypeStruct(dims, dtype)


def dot(a, b, dims):
    return lax.dot_general(a, b, (dims, ((), ())), preferred_element_type=F32)


def message_body(key_hbm, doc_hbm, out_ref, doc_ref, sems):
    tokens, width = key_hbm.shape
    copies = [
        pltpu.make_async_copy(doc_hbm, doc_ref, sems.at[0]),
        pltpu.make_async_copy(key_hbm, out_ref.at[pl.ds(0, tokens)], sems.at[1]),
    ]
    for copy in copies:
        copy.start()
    copies[0].wait()
    plus = doc_ref[...] + 1
    high = plus // DOC_BASE
    digits = jnp.concatenate([plus - high * DOC_BASE, high], 1).astype(F32)
    digits = jnp.broadcast_to(digits, (LABEL_ROWS, 2 * tokens)).astype(BF16)
    out_ref[tokens:, : 2 * tokens] = digits
    if width > 2 * tokens:
        out_ref[tokens:, 2 * tokens :] = jnp.zeros((LABEL_ROWS, width - 2 * tokens), BF16)
    copies[1].wait()


def docs_of(message_ref, tokens):
    codes = message_ref[tokens:, : 2 * tokens].astype(F32)[0:1]
    return codes[:, :tokens] + DOC_BASE * codes[:, tokens:] - 1.0


def column_of(row, eye):
    return jnp.sum(jnp.where(eye, row, 0.0), axis=1, keepdims=True)


def probs_body(q_ref, g_ref, k_ref, prior_ref, pt_ref, back_ref, own_ref):
    tokens = q_ref.shape[0]
    u = lax.broadcasted_iota(jnp.int32, (tokens, tokens), 0)
    t = lax.broadcasted_iota(jnp.int32, (tokens, tokens), 1)
    eye = u == t
    own_docs = docs_of(k_ref, tokens)
    prior_ok = column_of(docs_of(prior_ref, tokens), eye) == own_docs
    own_ok = (column_of(own_docs, eye) == own_docs) & (u <= t)
    prior_ok = jnp.concatenate([prior_ok] * GROUP, 1)
    own_ok = jnp.concatenate([own_ok] * GROUP, 1)
    scale = 1.0 / math.sqrt(HEAD_DIM)
    for g in range(KV_HEADS):
        heads = [slice((g * GROUP + r) * HEAD_DIM, (g * GROUP + r + 1) * HEAD_DIM) for r in range(GROUP)]
        col = slice(g * HEAD_DIM, (g + 1) * HEAD_DIM)
        q4 = jnp.concatenate([q_ref[:, h] for h in heads], 0)
        g4 = jnp.concatenate([g_ref[:, h] for h in heads], 0)
        sp = jnp.where(prior_ok, dot(prior_ref[:tokens, col], q4, ((1,), (1,))), MASKED)
        so = jnp.where(own_ok, dot(k_ref[:tokens, col], q4, ((1,), (1,))), MASKED)
        top = jnp.maximum(jnp.max(sp, 0, keepdims=True), jnp.max(so, 0, keepdims=True))
        ep = jnp.exp((sp - top) * scale)
        eo = jnp.exp((so - top) * scale)
        inv = 1.0 / (jnp.sum(ep, 0, keepdims=True) + jnp.sum(eo, 0, keepdims=True))
        pp = (ep * inv).astype(BF16)
        po = (eo * inv).astype(BF16)
        pt_ref[g, :tokens, :] = pp
        pt_ref[g, tokens:, :] = po
        back_ref[:, col] = dot(pp, g4, ((1,), (0,))).astype(BF16)
        own_ref[:, col] = dot(po, g4, ((1,), (0,)))


def copy_body(in_ref, out_ref):
    out_ref[...] = in_ref[...]


def attend_body(blocks, pt_ref, value_ref, prior_ref, plan_ref, out_ref):
    tokens = pt_ref.shape[1] // 2
    rows = tokens // blocks
    owners = out_ref.shape[0]
    data = KV_HEADS * GROUP * rows
    me = lax.axis_index("dp")
    if owners > blocks:
        out_ref[...] = jnp.zeros(out_ref.shape, BF16)
    slots = [plan_ref[j] ^ me for j in range(blocks)]
    for j in range(blocks):
        out_ref[slots[j], data:, :] = jnp.full((LABEL_ROWS, LANES), j + 1, F32).astype(BF16)
    for g in range(KV_HEADS):
        col = slice(g * HEAD_DIM, (g + 1) * HEAD_DIM)
        att = dot(pt_ref[g, :tokens, :], prior_ref[:, col], ((0,), (0,)))
        att = att + dot(pt_ref[g, tokens:, :], value_ref[:, col], ((0,), (0,)))
        att = att.astype(BF16)
        for r in range(GROUP):
            first = (g * GROUP + r) * rows
            for j in range(blocks):
                at = r * tokens + j * rows
                out_ref[slots[j], first : first + rows, :] = att[at : at + rows]


def place_body(blocks, *refs):
    *arrived, out_hbm, done_ref, wide_ref, sems = refs
    done_ref[...] = jnp.zeros(done_ref.shape, F32)
    rows = out_hbm.shape[0] // blocks
    heads = out_hbm.shape[1] // LANES
    labels = [jnp.max(a[heads * rows :, :].astype(F32)).astype(jnp.int32) for a in arrived]
    copies = []
    for i, a in enumerate(arrived):
        first = pl.multiple_of(jnp.maximum(labels[i] - 1, 0) * rows, rows)
        copies.append(pltpu.make_async_copy(wide_ref.at[i], out_hbm.at[pl.ds(first, rows)], sems.at[i]))

        @pl.when(labels[i] > 0)
        def _():
            for h in range(heads):
                wide_ref[i, :, h * LANES : (h + 1) * LANES] = a[h * rows : (h + 1) * rows, :]
            copies[i].start()

    for i, copy in enumerate(copies):

        @pl.when(labels[i] > 0)
        def _():
            copy.wait()


def split_body(reduced, places, chips, in_hbm, q_hbm, g_hbm, v_hbm, *refs):
    spread = len(places)
    outs, (q_ref, g_ref, v_ref, in_ref, sems) = refs[:spread], refs[spread:]
    copies = [
        pltpu.make_async_copy(src, dst, sems.at[i])
        for i, (src, dst) in enumerate(((in_hbm, in_ref), (q_hbm, q_ref), (g_hbm, g_ref), (v_hbm, v_ref)))
    ]
    for copy in copies:
        copy.start()
    sub = in_ref.shape[1] // (spread * len(reduced))
    core, x, z, y = chip_at()
    reps = lax.axis_size("rep")
    copies[0].wait()
    for k, (kx, kz, ky) in enumerate(places):
        for m, (mx, mz, my) in enumerate(reduced):
            first = (z ^ kz ^ mz) * chips + (x ^ kx ^ mx) * reps + (y ^ ky ^ my)
            first = pl.multiple_of(first * sub, sub)
            outs[k][m * sub : (m + 1) * sub, :] = in_ref[:, pl.ds(first, sub)].T
    for copy in copies[1:]:
        copy.wait()


def both_body(own_ref, ret_ref, out_ref):
    out_ref[...] = (own_ref[...] + ret_ref[...].astype(F32)).astype(BF16)


def product_body(cross, *refs):
    *ins, out_ref = refs
    count = len(ins) // 2
    half = out_ref.shape[1]
    core = chip_at()[0] ^ cross
    cols = pl.ds(pl.multiple_of(core * half, half), half)
    a = jnp.concatenate([ref[...] for ref in ins[:count]], 1)
    b = jnp.concatenate([ref[:, cols] for ref in ins[count:]], 0)
    out_ref[...] = dot(a, b, ((1,), (0,))).astype(out_ref.dtype)


def add_body(own_ref, cross_ref, *outs):
    sub = outs[0].shape[0]
    for m, out in enumerate(outs):
        rows = slice(m * sub, (m + 1) * sub)
        out[...] = (own_ref[rows, :] + cross_ref[rows, :].astype(F32)).astype(out.dtype)


def sum_body(*refs):
    *terms, out_ref = refs
    total = terms[0][...]
    for term in terms[1:]:
        total = total + term[...].astype(F32)
    out_ref[...] = total.astype(BF16)


def spread_body(places, resumed, *refs):
    count = len(places)
    mine, other = refs[:count], refs[count : 2 * count]
    *dones, wide_ref, sems = refs[2 * count + resumed :]
    out_hbm, *dones = dones
    for done_ref in dones:
        done_ref[...] = jnp.zeros(done_ref.shape, F32)
    sub, half = mine[0].shape
    core, x, _, y = chip_at()
    q = x * lax.axis_size("rep") + y
    copies = []
    for i, k in enumerate(places):
        for ref, at in ((mine[i], core), (other[i], core ^ 1)):
            wide_ref[i, :, pl.ds(pl.multiple_of(at * half, half), half)] = ref[...].astype(F32)
        rows = pl.ds(pl.multiple_of((q ^ k) * sub, sub), sub)
        copies.append(pltpu.make_async_copy(wide_ref.at[i], out_hbm.at[rows], sems.at[i]))
        copies[i].start()
    for copy in copies:
        copy.wait()


def weight_by_collectives(input_rows, grad_parts):
    own_grad, returned = grad_parts()
    grad_values = (own_grad + returned.astype(F32)).astype(BF16)
    term = jnp.einsum("tc,tf->cf", input_rows, grad_values, preferred_element_type=F32).astype(BF16)
    part = lax.psum_scatter(term, "ctx", scatter_dimension=0, tiled=True).astype(F32)
    return lax.psum(part, ("dp", "rep"))


def weight_by_collectives(input_rows, own_grad, returned):
    grad_values = (own_grad + returned.astype(F32)).astype(BF16)
    term = jnp.einsum("tc,tf->cf", input_rows, grad_values, preferred_element_type=F32).astype(BF16)
    part = lax.psum_scatter(term, "ctx", scatter_dimension=0, tiled=True).astype(F32)
    return lax.psum(part, ("dp", "rep"))


def local(inputs, queries, keys, values, grad_out, doc_ids, plan):
    tokens, width = inputs.shape[1:]
    q_width = queries.shape[2]
    kv_width = keys.shape[2]
    half = kv_width // CORES
    shards = ("ctx", "rep")
    micro, owners, reps = (lax.axis_size(axis) for axis in ("dp", "ctx", "rep"))
    chips = micro // CORES * reps
    blocks = plan.shape[1]
    rows = tokens // blocks

    places = [(kx, kz, 0) for kx in range(micro // CORES) for kz in range(2)]
    reduced = [(0, 2 * mz, my) for mz in range(owners // 2) for my in range(reps)]
    every = ("dp", "ctx", "rep")

    def away(value, x, z, y):
        return swap(value, every, (x * CORES * owners + z) * reps + y)

    sub = width // (len(places) * len(reduced))
    by_chips = sub % LANES == 0

    (message,) = call(
        message_body,
        [shape(tokens + LABEL_ROWS, kv_width)],
        [keys[0], doc_ids],
        hbm_in=(0, 1),
        scratch=[pltpu.VMEM(doc_ids.shape, jnp.int32), pltpu.SemaphoreType.DMA((2,))],
    )
    prior = from_behind(message, shards, 1)

    if by_chips:
        *pieces, q_rows, g_rows, value_rows = call(
            functools.partial(split_body, reduced, places, chips),
            [shape(len(reduced) * sub, tokens)] * len(places) + [shape(tokens, q_width)] * 2 + [shape(tokens, kv_width)],
            [inputs[0], queries[0], grad_out[0], values[0]],
            hbm_in=(0, 1, 2, 3),
            scratch=[pltpu.VMEM((tokens, width), BF16), pltpu.SemaphoreType.DMA((4,))],
        )

        def gather(value_of):
            far_first = [away(value_of(k), *place) for k, place in reversed([*enumerate(places)]) if k]
            return far_first + [value_of(0)]

        mine_in = gather(lambda k: pieces[k])
    else:
        q_rows, g_rows, value_rows = queries[0], grad_out[0], values[0]

    probs, back, own = call(
        probs_body,
        [
            shape(KV_HEADS, 2 * tokens, GROUP * tokens),
            shape(tokens, kv_width),
            shape(tokens, kv_width, dtype=F32),
        ],
        [q_rows, g_rows, message, prior],
        weight=100,
    )
    returned = from_behind(back, shards, -1)
    prior_values = from_behind(value_rows, shards, 1)
    if by_chips:
        (grad_values,) = call(both_body, [shape(tokens, kv_width)], [own, returned], deps=mine_in[1:3])
        grads = gather(lambda k: grad_values)
        factors = [*mine_in, *grads]
        (cross,) = call(functools.partial(product_body, 1), [shape(len(reduced) * sub, half)], factors, deps=[prior_values])
        (kept,) = call(
            functools.partial(product_body, 0), [shape(len(reduced) * sub, half, dtype=F32)], factors
        )
        partial = call(
            add_body,
            [shape(sub, half, dtype=F32)] + [shape(sub, half)] * (len(reduced) - 1),
            [kept, swap(cross, "dp", 1)],
        )
        arrived = [away(partial[m], *reduced[m]) for m in (*range(2, len(reduced)), 1)]

    (outgoing,) = call(
        functools.partial(attend_body, blocks),
        [shape(micro, (q_width // LANES) * rows + LABEL_ROWS, LANES)],
        [probs, value_rows, prior_values, plan[0]],
        weight=100,
        deps=[partial[0]] if by_chips else [],
    )
    arrived_out = [outgoing[0]] + [swap(outgoing[m], "dp", m) for m in range(1, micro)]

    token = shape(8, LANES, dtype=F32)
    placed, in_place = call(
        functools.partial(place_body, blocks),
        [shape(tokens, q_width), token],
        arrived_out,
        hbm_out=(0,),
        scratch=[pltpu.VMEM((micro, rows, q_width), BF16), pltpu.SemaphoreType.DMA((micro,))],
        weight=2,
    )
    if by_chips:
        (total,) = call(sum_body, [shape(sub, half)], [partial[0], *arrived], deps=[outgoing])
        sums = [away(total, k // reps, 0, k % reps) for k in reversed(range(1, chips))]
        sums = [total, *reversed(sums)]
        others = {}

        def spread(chosen, so_far=(), weight=0):
            pieces = [sums[k] for k in chosen] + [others[k] for k in chosen]
            return call(
                functools.partial(spread_body, chosen, len(so_far)),
                [shape(chips * sub, kv_width, dtype=F32)] + [token] * (not so_far),
                [*pieces, *so_far],
                weight=weight,
                hbm_in=(len(pieces),),
                hbm_out=(0,),
                scratch=[pltpu.VMEM((len(chosen), sub, kv_width), F32), pltpu.SemaphoreType.DMA((len(chosen),))],
                alias={len(pieces): 0} if so_far else {},
            )

        early = [k for k in range(chips) if k % reps == 0]
        late = [k for k in reversed(range(chips)) if k % reps]
        for k in early:
            others[k] = swap(sums[k], "dp", 1)
        weight_grad, written = spread(early, weight=2)
        for k in late:
            (sums[k],) = call(copy_body, [shape(sub, half)], [sums[k]], deps=[written, in_place])
            others[k] = swap(sums[k], "dp", 1)
        (weight_grad,) = spread(late, [weight_grad])
    else:
        weight_grad = weight_by_collectives(inputs[0], own, returned)
    return (placed[None], weight_grad)


def solution(mesh):
    rows = P("dp", ("ctx", "rep"), None)
    ids = P("dp", ("ctx", "rep"))
    return jax.shard_map(
        local,
        mesh=mesh,
        in_specs=(rows, rows, rows, rows, rows, ids, ids),
        out_specs=(rows, P("ctx", None)),
        check_vma=False,
    )
```

```python
import functools
import math

import jax
import jax.numpy as jnp
from jax import lax
from jax.experimental import pallas as pl
from jax.experimental.pallas import tpu as pltpu
from jax.sharding import PartitionSpec as P

HEAD_DIM = 128
KV_HEADS = 4
GROUP = 4
CORES = 2
LANES = 128
LABEL_ROWS = 16
DOC_BASE = 128
MASKED = -1e30
BF16 = jnp.bfloat16
F32 = jnp.float32


def from_behind(value, axis, by):
    devices = lax.axis_size(axis)
    return lax.ppermute(value, axis, [(i, (i + by) % devices) for i in range(devices)])


def open_ended(value, axis, by):
    devices = lax.axis_size(axis)
    pairs = [(i, i + by) for i in range(devices) if 0 <= i + by < devices]
    return lax.ppermute(value, axis, pairs)


def swap(value, axis, mask):
    devices = lax.axis_size(axis)
    return lax.ppermute(value, axis, [(i, i ^ mask) for i in range(devices)])


def chip_at():
    dp = lax.axis_index("dp")
    return dp % CORES, dp // CORES, lax.axis_index("ctx"), lax.axis_index("rep")


def vmem():
    return pl.BlockSpec(memory_space=pltpu.VMEM)


def smem():
    return pl.BlockSpec(memory_space=pltpu.SMEM)


def call(body, outs, ins, weight=0, deps=(), hbm_in=(), hbm_out=(), scratch=(), alias={}):
    space = pl.BlockSpec(memory_space=pltpu.HBM)
    ins_at = [smem() if a.dtype == jnp.int32 and a.ndim == 1 else vmem() for a in ins]
    ins_at = [space if i in hbm_in else at for i, at in enumerate(ins_at)]
    skip = len(deps)
    ins = [pltpu.with_memory_space_constraint(a, pltpu.HBM) if i in hbm_in else a for i, a in enumerate(ins)]
    return pl.pallas_call(
        lambda *refs: body(*refs[skip:]),
        out_shape=[pltpu.HBM(o.shape, o.dtype) if i in hbm_out else o for i, o in enumerate(outs)],
        in_specs=[space] * skip + ins_at,
        out_specs=[space if i in hbm_out else vmem() for i in range(len(outs))],
        scratch_shapes=list(scratch),
        input_output_aliases={skip + i: o for i, o in alias.items()},
        cost_estimate=pl.CostEstimate(flops=weight * 10**9, bytes_accessed=0, transcendentals=0),
        compiler_params=pltpu.CompilerParams(vmem_limit_bytes=32 * 2**20),
    )(*deps, *ins)


def shape(*dims, dtype=BF16):
    return jax.ShapeDtypeStruct(dims, dtype)


def dot(a, b, dims):
    return lax.dot_general(a, b, (dims, ((), ())), preferred_element_type=F32)


def message_body(key_hbm, doc_hbm, out_ref, doc_ref, sems):
    tokens, width = key_hbm.shape
    copies = [
        pltpu.make_async_copy(doc_hbm, doc_ref, sems.at[0]),
        pltpu.make_async_copy(key_hbm, out_ref.at[pl.ds(0, tokens)], sems.at[1]),
    ]
    for copy in copies:
        copy.start()
    copies[0].wait()
    plus = doc_ref[...] + 1
    high = plus // DOC_BASE
    digits = jnp.concatenate([plus - high * DOC_BASE, high], 1).astype(F32)
    digits = jnp.broadcast_to(digits, (LABEL_ROWS, 2 * tokens)).astype(BF16)
    out_ref[tokens:, : 2 * tokens] = digits
    if width > 2 * tokens:
        out_ref[tokens:, 2 * tokens :] = jnp.zeros((LABEL_ROWS, width - 2 * tokens), BF16)
    copies[1].wait()


def docs_of(message_ref, tokens):
    codes = message_ref[tokens:, : 2 * tokens].astype(F32)[0:1]
    return codes[:, :tokens] + DOC_BASE * codes[:, tokens:] - 1.0


def column_of(row, eye):
    return jnp.sum(jnp.where(eye, row, 0.0), axis=1, keepdims=True)


def probs_body(q_ref, g_ref, k_ref, prior_ref, pt_ref, back_ref, own_ref):
    tokens = q_ref.shape[0]
    u = lax.broadcasted_iota(jnp.int32, (tokens, tokens), 0)
    t = lax.broadcasted_iota(jnp.int32, (tokens, tokens), 1)
    eye = u == t
    own_docs = docs_of(k_ref, tokens)
    first = (lax.axis_index("ctx") == 0) & (lax.axis_index("rep") == 0)
    prior_docs = jnp.where(first, -1.0, docs_of(prior_ref, tokens))
    prior_ok = column_of(prior_docs, eye) == own_docs
    own_ok = (column_of(own_docs, eye) == own_docs) & (u <= t)
    prior_ok = jnp.concatenate([prior_ok] * GROUP, 1)
    own_ok = jnp.concatenate([own_ok] * GROUP, 1)
    scale = 1.0 / math.sqrt(HEAD_DIM)
    for g in range(KV_HEADS):
        heads = [slice((g * GROUP + r) * HEAD_DIM, (g * GROUP + r + 1) * HEAD_DIM) for r in range(GROUP)]
        col = slice(g * HEAD_DIM, (g + 1) * HEAD_DIM)
        q4 = jnp.concatenate([q_ref[:, h] for h in heads], 0)
        g4 = jnp.concatenate([g_ref[:, h] for h in heads], 0)
        sp = jnp.where(prior_ok, dot(prior_ref[:tokens, col], q4, ((1,), (1,))), MASKED)
        so = jnp.where(own_ok, dot(k_ref[:tokens, col], q4, ((1,), (1,))), MASKED)
        top = jnp.maximum(jnp.max(sp, 0, keepdims=True), jnp.max(so, 0, keepdims=True))
        ep = jnp.exp((sp - top) * scale)
        eo = jnp.exp((so - top) * scale)
        inv = 1.0 / (jnp.sum(ep, 0, keepdims=True) + jnp.sum(eo, 0, keepdims=True))
        pp = (ep * inv).astype(BF16)
        po = (eo * inv).astype(BF16)
        pt_ref[g, :tokens, :] = pp
        pt_ref[g, tokens:, :] = po
        back_ref[:, col] = dot(pp, g4, ((1,), (0,))).astype(BF16)
        own_ref[:, col] = dot(po, g4, ((1,), (0,)))


def copy_body(in_ref, out_ref):
    out_ref[...] = in_ref[...]


def attend_body(blocks, pt_ref, value_ref, prior_ref, plan_ref, out_ref):
    tokens = pt_ref.shape[1] // 2
    rows = tokens // blocks
    owners = out_ref.shape[0]
    data = KV_HEADS * GROUP * rows
    me = lax.axis_index("dp")
    if owners > blocks:
        out_ref[...] = jnp.zeros(out_ref.shape, BF16)
    slots = [plan_ref[j] ^ me for j in range(blocks)]
    for j in range(blocks):
        out_ref[slots[j], data:, :] = jnp.full((LABEL_ROWS, LANES), j + 1, F32).astype(BF16)
    for g in range(KV_HEADS):
        col = slice(g * HEAD_DIM, (g + 1) * HEAD_DIM)
        att = dot(pt_ref[g, :tokens, :], prior_ref[:, col], ((0,), (0,)))
        att = att + dot(pt_ref[g, tokens:, :], value_ref[:, col], ((0,), (0,)))
        att = att.astype(BF16)
        for r in range(GROUP):
            first = (g * GROUP + r) * rows
            for j in range(blocks):
                at = r * tokens + j * rows
                out_ref[slots[j], first : first + rows, :] = att[at : at + rows]


def place_body(blocks, *refs):
    *arrived, out_hbm, done_ref, wide_ref, sems = refs
    done_ref[...] = jnp.zeros(done_ref.shape, F32)
    rows = out_hbm.shape[0] // blocks
    heads = out_hbm.shape[1] // LANES
    labels = [jnp.max(a[heads * rows :, :].astype(F32)).astype(jnp.int32) for a in arrived]
    copies = []
    for i, a in enumerate(arrived):
        first = pl.multiple_of(jnp.maximum(labels[i] - 1, 0) * rows, rows)
        copies.append(pltpu.make_async_copy(wide_ref.at[i], out_hbm.at[pl.ds(first, rows)], sems.at[i]))

        @pl.when(labels[i] > 0)
        def _():
            for h in range(heads):
                wide_ref[i, :, h * LANES : (h + 1) * LANES] = a[h * rows : (h + 1) * rows, :]
            copies[i].start()

    for i, copy in enumerate(copies):

        @pl.when(labels[i] > 0)
        def _():
            copy.wait()


def split_body(reduced, places, chips, in_hbm, q_hbm, g_hbm, v_hbm, *refs):
    spread = len(places)
    outs, (q_ref, g_ref, v_ref, in_ref, sems) = refs[:spread], refs[spread:]
    copies = [
        pltpu.make_async_copy(src, dst, sems.at[i])
        for i, (src, dst) in enumerate(((in_hbm, in_ref), (q_hbm, q_ref), (g_hbm, g_ref), (v_hbm, v_ref)))
    ]
    for copy in copies:
        copy.start()
    sub = in_ref.shape[1] // (spread * len(reduced))
    core, x, z, y = chip_at()
    reps = lax.axis_size("rep")
    copies[0].wait()
    for k, (kx, kz, ky) in enumerate(places):
        for m, (mx, mz, my) in enumerate(reduced):
            first = (z ^ kz ^ mz) * chips + (x ^ kx ^ mx) * reps + (y ^ ky ^ my)
            first = pl.multiple_of(first * sub, sub)
            outs[k][m * sub : (m + 1) * sub, :] = in_ref[:, pl.ds(first, sub)].T
    for copy in copies[1:]:
        copy.wait()


def both_body(own_ref, ret_ref, out_ref):
    out_ref[...] = (own_ref[...] + ret_ref[...].astype(F32)).astype(BF16)


def product_body(cross, rows, *refs):
    *ins, out_ref = refs
    count = len(ins) // 2
    half = out_ref.shape[1]
    core = chip_at()[0] ^ cross
    cols = pl.ds(pl.multiple_of(core * half, half), half)
    a = jnp.concatenate([ref[rows, :] for ref in ins[:count]], 1)
    b = jnp.concatenate([ref[:, cols] for ref in ins[count:]], 0)
    out_ref[...] = dot(a, b, ((1,), (0,))).astype(out_ref.dtype)


def add_body(own_ref, cross_ref, *outs):
    sub = outs[0].shape[0]
    for m, out in enumerate(outs):
        rows = slice(m * sub, (m + 1) * sub)
        out[...] = (own_ref[rows, :] + cross_ref[rows, :].astype(F32)).astype(out.dtype)


def sum_body(*refs):
    *terms, out_ref = refs
    total = terms[0][...]
    for term in terms[1:]:
        total = total + term[...].astype(F32)
    out_ref[...] = total.astype(BF16)


def spread_body(places, resumed, *refs):
    count = len(places)
    mine, other = refs[:count], refs[count : 2 * count]
    *dones, wide_ref, sems = refs[2 * count + resumed :]
    out_hbm, *dones = dones
    for done_ref in dones:
        done_ref[...] = jnp.zeros(done_ref.shape, F32)
    sub, half = mine[0].shape
    core, x, _, y = chip_at()
    q = x * lax.axis_size("rep") + y
    copies = []
    for i, k in enumerate(places):
        for ref, at in ((mine[i], core), (other[i], core ^ 1)):
            wide_ref[i, :, pl.ds(pl.multiple_of(at * half, half), half)] = ref[...].astype(F32)
        rows = pl.ds(pl.multiple_of((q ^ k) * sub, sub), sub)
        copies.append(pltpu.make_async_copy(wide_ref.at[i], out_hbm.at[rows], sems.at[i]))
        copies[i].start()
    for copy in copies:
        copy.wait()


def weight_by_collectives(input_rows, grad_parts):
    own_grad, returned = grad_parts()
    grad_values = (own_grad + returned.astype(F32)).astype(BF16)
    term = jnp.einsum("tc,tf->cf", input_rows, grad_values, preferred_element_type=F32).astype(BF16)
    part = lax.psum_scatter(term, "ctx", scatter_dimension=0, tiled=True).astype(F32)
    return lax.psum(part, ("dp", "rep"))


def weight_by_collectives(input_rows, own_grad, returned):
    grad_values = (own_grad + returned.astype(F32)).astype(BF16)
    term = jnp.einsum("tc,tf->cf", input_rows, grad_values, preferred_element_type=F32).astype(BF16)
    part = lax.psum_scatter(term, "ctx", scatter_dimension=0, tiled=True).astype(F32)
    return lax.psum(part, ("dp", "rep"))


def local(inputs, queries, keys, values, grad_out, doc_ids, plan):
    tokens, width = inputs.shape[1:]
    q_width = queries.shape[2]
    kv_width = keys.shape[2]
    half = kv_width // CORES
    shards = ("ctx", "rep")
    micro, owners, reps = (lax.axis_size(axis) for axis in ("dp", "ctx", "rep"))
    chips = micro // CORES * reps
    blocks = plan.shape[1]
    rows = tokens // blocks

    places = [(kx, kz, 0) for kx in range(micro // CORES) for kz in range(2)]
    reduced = [(0, 2 * mz, my) for mz in range(owners // 2) for my in range(reps)]
    every = ("dp", "ctx", "rep")

    def away(value, x, z, y):
        return swap(value, every, (x * CORES * owners + z) * reps + y)

    sub = width // (len(places) * len(reduced))
    by_chips = sub % LANES == 0

    (message,) = call(
        message_body,
        [shape(tokens + LABEL_ROWS, kv_width)],
        [keys[0], doc_ids],
        hbm_in=(0, 1),
        scratch=[pltpu.VMEM(doc_ids.shape, jnp.int32), pltpu.SemaphoreType.DMA((2,))],
    )
    prior = from_behind(message, shards, 1)

    if by_chips:
        *pieces, q_rows, g_rows, value_rows = call(
            functools.partial(split_body, reduced, places, chips),
            [shape(len(reduced) * sub, tokens)] * len(places) + [shape(tokens, q_width)] * 2 + [shape(tokens, kv_width)],
            [inputs[0], queries[0], grad_out[0], values[0]],
            hbm_in=(0, 1, 2, 3),
            scratch=[pltpu.VMEM((tokens, width), BF16), pltpu.SemaphoreType.DMA((4,))],
        )

        def gather(value_of):
            far_first = [away(value_of(k), *place) for k, place in reversed([*enumerate(places)]) if k]
            return far_first + [value_of(0)]

        mine_in = gather(lambda k: pieces[k])
    else:
        q_rows, g_rows, value_rows = queries[0], grad_out[0], values[0]

    probs, back, own = call(
        probs_body,
        [
            shape(KV_HEADS, 2 * tokens, GROUP * tokens),
            shape(tokens, kv_width),
            shape(tokens, kv_width, dtype=F32),
        ],
        [q_rows, g_rows, message, prior],
        weight=100,
    )
    returned = from_behind(back, shards, -1)
    prior_values = open_ended(value_rows, shards, 1)
    if by_chips:
        (grad_values,) = call(both_body, [shape(tokens, kv_width)], [own, returned], deps=mine_in[1:3])
        grads = gather(lambda k: grad_values)
        factors = [*mine_in, *grads]

        def products(first, last, deps):
            rows = slice(first * sub, last * sub)
            many = (last - first) * sub
            (cross,) = call(functools.partial(product_body, 1, rows), [shape(many, half)], factors, deps=deps)
            (kept,) = call(
                functools.partial(product_body, 0, rows), [shape(many, half, dtype=F32)], factors, deps=deps, weight=3
            )
            return call(
                add_body,
                [shape(sub, half, dtype=BF16 if m else F32) for m in range(first, last)],
                [kept, swap(cross, "dp", 1)],
            )

        far = products(2, len(reduced), [prior_values])
        near = products(0, 2, [far[0]])
        partial = [*near, *far]
        arrived = [away(partial[m], *reduced[m]) for m in (*range(2, len(reduced)), 1)]

    (outgoing,) = call(
        functools.partial(attend_body, blocks),
        [shape(micro, (q_width // LANES) * rows + LABEL_ROWS, LANES)],
        [probs, value_rows, prior_values, plan[0]],
        weight=100,
        deps=[partial[0]] if by_chips else [],
    )
    arrived_out = [outgoing[0]] + [swap(outgoing[m], "dp", m) for m in range(1, micro)]

    token = shape(8, LANES, dtype=F32)
    placed, in_place = call(
        functools.partial(place_body, blocks),
        [shape(tokens, q_width), token],
        arrived_out,
        hbm_out=(0,),
        scratch=[pltpu.VMEM((micro, rows, q_width), BF16), pltpu.SemaphoreType.DMA((micro,))],
        weight=2,
    )
    if by_chips:
        (total,) = call(sum_body, [shape(sub, half)], [partial[0], *arrived], deps=[outgoing])
        sums = [away(total, k // reps, 0, k % reps) for k in reversed(range(1, chips))]
        sums = [total, *reversed(sums)]
        others = {}

        def spread(chosen, so_far=(), weight=0):
            pieces = [sums[k] for k in chosen] + [others[k] for k in chosen]
            return call(
                functools.partial(spread_body, chosen, len(so_far)),
                [shape(chips * sub, kv_width, dtype=F32)] + [token] * (not so_far),
                [*pieces, *so_far],
                weight=weight,
                hbm_in=(len(pieces),),
                hbm_out=(0,),
                scratch=[pltpu.VMEM((len(chosen), sub, kv_width), F32), pltpu.SemaphoreType.DMA((len(chosen),))],
                alias={len(pieces): 0} if so_far else {},
            )

        early = [k for k in range(chips) if k % reps == 0]
        late = [k for k in reversed(range(chips)) if k % reps]
        for k in early:
            others[k] = swap(sums[k], "dp", 1)
        weight_grad, written = spread(early, weight=2)
        for k in late:
            (sums[k],) = call(copy_body, [shape(sub, half)], [sums[k]], deps=[written, in_place])
            others[k] = swap(sums[k], "dp", 1)
        (weight_grad,) = spread(late, [weight_grad])
    else:
        weight_grad = weight_by_collectives(inputs[0], own, returned)
    return (placed[None], weight_grad)


def solution(mesh):
    rows = P("dp", ("ctx", "rep"), None)
    ids = P("dp", ("ctx", "rep"))
    return jax.shard_map(
        local,
        mesh=mesh,
        in_specs=(rows, rows, rows, rows, rows, ids, ids),
        out_specs=(rows, P("ctx", None)),
        check_vma=False,
    )
```

```python
import functools
import math

import jax
import jax.numpy as jnp
from jax import lax
from jax.experimental import pallas as pl
from jax.experimental.pallas import tpu as pltpu
from jax.sharding import PartitionSpec as P

HEAD_DIM = 128
KV_HEADS = 4
GROUP = 4
CORES = 2
LANES = 128
LABEL_ROWS = 16
DOC_BASE = 128
MASKED = -1e30
BF16 = jnp.bfloat16
F32 = jnp.float32


def from_behind(value, axis, by):
    devices = lax.axis_size(axis)
    return lax.ppermute(value, axis, [(i, (i + by) % devices) for i in range(devices)])


def open_ended(value, axis, by):
    devices = lax.axis_size(axis)
    pairs = [(i, i + by) for i in range(devices) if 0 <= i + by < devices]
    return lax.ppermute(value, axis, pairs)


def swap(value, axis, mask):
    devices = lax.axis_size(axis)
    return lax.ppermute(value, axis, [(i, i ^ mask) for i in range(devices)])


def chip_at():
    dp = lax.axis_index("dp")
    return dp % CORES, dp // CORES, lax.axis_index("ctx"), lax.axis_index("rep")


def vmem():
    return pl.BlockSpec(memory_space=pltpu.VMEM)


def smem():
    return pl.BlockSpec(memory_space=pltpu.SMEM)


def call(body, outs, ins, weight=0, deps=(), hbm_in=(), hbm_out=(), scratch=(), alias={}):
    space = pl.BlockSpec(memory_space=pltpu.HBM)
    ins_at = [smem() if a.dtype == jnp.int32 and a.ndim == 1 else vmem() for a in ins]
    ins_at = [space if i in hbm_in else at for i, at in enumerate(ins_at)]
    skip = len(deps)
    ins = [pltpu.with_memory_space_constraint(a, pltpu.HBM) if i in hbm_in else a for i, a in enumerate(ins)]
    return pl.pallas_call(
        lambda *refs: body(*refs[skip:]),
        out_shape=[pltpu.HBM(o.shape, o.dtype) if i in hbm_out else o for i, o in enumerate(outs)],
        in_specs=[space] * skip + ins_at,
        out_specs=[space if i in hbm_out else vmem() for i in range(len(outs))],
        scratch_shapes=list(scratch),
        input_output_aliases={skip + i: o for i, o in alias.items()},
        cost_estimate=pl.CostEstimate(flops=weight * 10**9, bytes_accessed=0, transcendentals=0),
        compiler_params=pltpu.CompilerParams(vmem_limit_bytes=32 * 2**20),
    )(*deps, *ins)


def shape(*dims, dtype=BF16):
    return jax.ShapeDtypeStruct(dims, dtype)


def dot(a, b, dims):
    return lax.dot_general(a, b, (dims, ((), ())), preferred_element_type=F32)


def message_body(key_hbm, doc_hbm, out_ref, doc_ref, sems):
    tokens, width = key_hbm.shape
    copies = [
        pltpu.make_async_copy(doc_hbm, doc_ref, sems.at[0]),
        pltpu.make_async_copy(key_hbm, out_ref.at[pl.ds(0, tokens)], sems.at[1]),
    ]
    for copy in copies:
        copy.start()
    copies[0].wait()
    plus = doc_ref[...] + 1
    high = plus // DOC_BASE
    digits = jnp.concatenate([plus - high * DOC_BASE, high], 1).astype(F32)
    digits = jnp.broadcast_to(digits, (LABEL_ROWS, 2 * tokens)).astype(BF16)
    out_ref[tokens:, : 2 * tokens] = digits
    if width > 2 * tokens:
        out_ref[tokens:, 2 * tokens :] = jnp.zeros((LABEL_ROWS, width - 2 * tokens), BF16)
    copies[1].wait()


def docs_of(message_ref, tokens):
    codes = message_ref[tokens:, : 2 * tokens].astype(F32)[0:1]
    return codes[:, :tokens] + DOC_BASE * codes[:, tokens:] - 1.0


def column_of(row, eye):
    return jnp.sum(jnp.where(eye, row, 0.0), axis=1, keepdims=True)


def probs_body(q_ref, g_ref, k_ref, prior_ref, pt_ref, back_ref):
    tokens = q_ref.shape[0]
    u = lax.broadcasted_iota(jnp.int32, (tokens, tokens), 0)
    t = lax.broadcasted_iota(jnp.int32, (tokens, tokens), 1)
    eye = u == t
    own_docs = docs_of(k_ref, tokens)
    first = (lax.axis_index("ctx") == 0) & (lax.axis_index("rep") == 0)
    prior_docs = jnp.where(first, -1.0, docs_of(prior_ref, tokens))
    prior_ok = column_of(prior_docs, eye) == own_docs
    own_ok = (column_of(own_docs, eye) == own_docs) & (u <= t)
    prior_ok = jnp.concatenate([prior_ok] * GROUP, 1)
    own_ok = jnp.concatenate([own_ok] * GROUP, 1)
    scale = math.log2(math.e) / math.sqrt(HEAD_DIM)
    for g in range(KV_HEADS):
        heads = [slice((g * GROUP + r) * HEAD_DIM, (g * GROUP + r + 1) * HEAD_DIM) for r in range(GROUP)]
        col = slice(g * HEAD_DIM, (g + 1) * HEAD_DIM)
        q4 = jnp.concatenate([q_ref[:, h] for h in heads], 0)
        g4 = jnp.concatenate([g_ref[:, h] for h in heads], 0)
        sp = jnp.where(prior_ok, dot(prior_ref[:tokens, col], q4, ((1,), (1,))), MASKED)
        so = jnp.where(own_ok, dot(k_ref[:tokens, col], q4, ((1,), (1,))), MASKED)
        top = jnp.maximum(jnp.max(sp, 0, keepdims=True), jnp.max(so, 0, keepdims=True))
        ep = jnp.exp2((sp - top) * scale)
        eo = jnp.exp2((so - top) * scale)
        inv = 1.0 / (jnp.sum(ep, 0, keepdims=True) + jnp.sum(eo, 0, keepdims=True))
        pp = (ep * inv).astype(BF16)
        po = (eo * inv).astype(BF16)
        pt_ref[g, :tokens, :] = pp
        pt_ref[g, tokens:, :] = po
        back_ref[:, col] = dot(pp, g4, ((1,), (0,))).astype(BF16)


def own_body(pt_ref, g_ref, own_ref):
    tokens = g_ref.shape[0]
    for g in range(KV_HEADS):
        heads = [slice((g * GROUP + r) * HEAD_DIM, (g * GROUP + r + 1) * HEAD_DIM) for r in range(GROUP)]
        g4 = jnp.concatenate([g_ref[:, h] for h in heads], 0)
        own_ref[:, g * HEAD_DIM : (g + 1) * HEAD_DIM] = dot(pt_ref[g, tokens:, :], g4, ((1,), (0,)))


def copy_body(in_ref, out_ref):
    out_ref[...] = in_ref[...]


def attend_body(blocks, pt_ref, value_ref, prior_ref, plan_ref, out_ref):
    tokens = pt_ref.shape[1] // 2
    rows = tokens // blocks
    owners = out_ref.shape[0]
    data = KV_HEADS * GROUP * rows
    me = lax.axis_index("dp")
    if owners > blocks:
        out_ref[...] = jnp.zeros(out_ref.shape, BF16)
    slots = [plan_ref[j] ^ me for j in range(blocks)]
    for j in range(blocks):
        out_ref[slots[j], data:, :] = jnp.full((LABEL_ROWS, LANES), j + 1, F32).astype(BF16)
    for g in range(KV_HEADS):
        col = slice(g * HEAD_DIM, (g + 1) * HEAD_DIM)
        att = dot(pt_ref[g, :tokens, :], prior_ref[:, col], ((0,), (0,)))
        att = att + dot(pt_ref[g, tokens:, :], value_ref[:, col], ((0,), (0,)))
        att = att.astype(BF16)
        for r in range(GROUP):
            first = (g * GROUP + r) * rows
            for j in range(blocks):
                at = r * tokens + j * rows
                out_ref[slots[j], first : first + rows, :] = att[at : at + rows]


def place_body(blocks, *refs):
    *arrived, out_hbm, done_ref, wide_ref, sems = refs
    done_ref[...] = jnp.zeros(done_ref.shape, F32)
    rows = out_hbm.shape[0] // blocks
    heads = out_hbm.shape[1] // LANES
    labels = [jnp.max(a[heads * rows :, :].astype(F32)).astype(jnp.int32) for a in arrived]
    copies = []
    for i, a in enumerate(arrived):
        first = pl.multiple_of(jnp.maximum(labels[i] - 1, 0) * rows, rows)
        copies.append(pltpu.make_async_copy(wide_ref.at[i], out_hbm.at[pl.ds(first, rows)], sems.at[i]))

        @pl.when(labels[i] > 0)
        def _():
            for h in range(heads):
                wide_ref[i, :, h * LANES : (h + 1) * LANES] = a[h * rows : (h + 1) * rows, :]
            copies[i].start()

    for i, copy in enumerate(copies):

        @pl.when(labels[i] > 0)
        def _():
            copy.wait()


def split_body(reduced, places, chips, in_hbm, q_hbm, g_hbm, v_hbm, *refs):
    spread = len(places)
    outs, (q_ref, g_ref, v_ref, in_ref, sems) = refs[:spread], refs[spread:]
    copies = [
        pltpu.make_async_copy(src, dst, sems.at[i])
        for i, (src, dst) in enumerate(((in_hbm, in_ref), (q_hbm, q_ref), (g_hbm, g_ref), (v_hbm, v_ref)))
    ]
    for copy in copies:
        copy.start()
    sub = in_ref.shape[1] // (spread * len(reduced))
    core, x, z, y = chip_at()
    reps = lax.axis_size("rep")
    copies[0].wait()
    for k, (kx, kz, ky) in enumerate(places):
        for m, (mx, mz, my) in enumerate(reduced):
            first = (z ^ kz ^ mz) * chips + (x ^ kx ^ mx) * reps + (y ^ ky ^ my)
            first = pl.multiple_of(first * sub, sub)
            outs[k][m * sub : (m + 1) * sub, :] = in_ref[:, pl.ds(first, sub)].T
    for copy in copies[1:]:
        copy.wait()


def both_body(own_ref, ret_ref, out_ref):
    out_ref[...] = (own_ref[...] + ret_ref[...].astype(F32)).astype(BF16)


def product_body(cross, rows, *refs):
    *ins, out_ref = refs
    count = len(ins) // 2
    half = out_ref.shape[1]
    core = chip_at()[0] ^ cross
    cols = pl.ds(pl.multiple_of(core * half, half), half)
    a = jnp.concatenate([ref[rows, :] for ref in ins[:count]], 1)
    b = jnp.concatenate([ref[:, cols] for ref in ins[count:]], 0)
    out_ref[...] = dot(a, b, ((1,), (0,))).astype(out_ref.dtype)


def add_body(own_ref, cross_ref, *outs):
    sub = outs[0].shape[0]
    for m, out in enumerate(outs):
        rows = slice(m * sub, (m + 1) * sub)
        out[...] = (own_ref[rows, :] + cross_ref[rows, :].astype(F32)).astype(out.dtype)


def sum_body(*refs):
    *terms, out_ref = refs
    total = terms[0][...]
    for term in terms[1:]:
        total = total + term[...].astype(F32)
    out_ref[...] = total.astype(BF16)


def spread_body(places, resumed, *refs):
    count = len(places)
    mine, other = refs[:count], refs[count : 2 * count]
    *dones, wide_ref, sems = refs[2 * count + resumed :]
    out_hbm, *dones = dones
    for done_ref in dones:
        done_ref[...] = jnp.zeros(done_ref.shape, F32)
    sub, half = mine[0].shape
    core, x, _, y = chip_at()
    q = x * lax.axis_size("rep") + y
    copies = []
    for i, k in enumerate(places):
        for ref, at in ((mine[i], core), (other[i], core ^ 1)):
            wide_ref[i, :, pl.ds(pl.multiple_of(at * half, half), half)] = ref[...].astype(F32)
        rows = pl.ds(pl.multiple_of((q ^ k) * sub, sub), sub)
        copies.append(pltpu.make_async_copy(wide_ref.at[i], out_hbm.at[rows], sems.at[i]))
        copies[i].start()
    for copy in copies:
        copy.wait()


def weight_by_collectives(input_rows, grad_parts):
    own_grad, returned = grad_parts()
    grad_values = (own_grad + returned.astype(F32)).astype(BF16)
    term = jnp.einsum("tc,tf->cf", input_rows, grad_values, preferred_element_type=F32).astype(BF16)
    part = lax.psum_scatter(term, "ctx", scatter_dimension=0, tiled=True).astype(F32)
    return lax.psum(part, ("dp", "rep"))


def weight_by_collectives(input_rows, own_grad, returned):
    grad_values = (own_grad + returned.astype(F32)).astype(BF16)
    term = jnp.einsum("tc,tf->cf", input_rows, grad_values, preferred_element_type=F32).astype(BF16)
    part = lax.psum_scatter(term, "ctx", scatter_dimension=0, tiled=True).astype(F32)
    return lax.psum(part, ("dp", "rep"))


def local(inputs, queries, keys, values, grad_out, doc_ids, plan):
    tokens, width = inputs.shape[1:]
    q_width = queries.shape[2]
    kv_width = keys.shape[2]
    half = kv_width // CORES
    shards = ("ctx", "rep")
    micro, owners, reps = (lax.axis_size(axis) for axis in ("dp", "ctx", "rep"))
    chips = micro // CORES * reps
    blocks = plan.shape[1]
    rows = tokens // blocks

    places = [(kx, kz, 0) for kx in range(micro // CORES) for kz in range(2)]
    reduced = [(0, 2 * mz, my) for mz in range(owners // 2) for my in range(reps)]
    every = ("dp", "ctx", "rep")

    def away(value, x, z, y):
        return swap(value, every, (x * CORES * owners + z) * reps + y)

    sub = width // (len(places) * len(reduced))
    by_chips = sub % LANES == 0

    (message,) = call(
        message_body,
        [shape(tokens + LABEL_ROWS, kv_width)],
        [keys[0], doc_ids],
        hbm_in=(0, 1),
        scratch=[pltpu.VMEM(doc_ids.shape, jnp.int32), pltpu.SemaphoreType.DMA((2,))],
    )
    prior = from_behind(message, shards, 1)

    if by_chips:
        *pieces, q_rows, g_rows, value_rows = call(
            functools.partial(split_body, reduced, places, chips),
            [shape(len(reduced) * sub, tokens)] * len(places) + [shape(tokens, q_width)] * 2 + [shape(tokens, kv_width)],
            [inputs[0], queries[0], grad_out[0], values[0]],
            hbm_in=(0, 1, 2, 3),
            scratch=[pltpu.VMEM((tokens, width), BF16), pltpu.SemaphoreType.DMA((4,))],
        )

        def gather(value_of):
            far_first = [away(value_of(k), *place) for k, place in reversed([*enumerate(places)]) if k]
            x, z = far_first[1:]
            return [far_first[0], z, x, value_of(0)]

        mine_in = gather(lambda k: pieces[k])
    else:
        q_rows, g_rows, value_rows = queries[0], grad_out[0], values[0]

    probs, back = call(
        probs_body,
        [shape(KV_HEADS, 2 * tokens, GROUP * tokens), shape(tokens, kv_width)],
        [q_rows, g_rows, message, prior],
        weight=100,
    )
    (own,) = call(own_body, [shape(tokens, kv_width, dtype=F32)], [probs, g_rows], weight=1)
    returned = from_behind(back, shards, -1)
    prior_values = open_ended(value_rows, shards, 1)
    if by_chips:
        (grad_values,) = call(both_body, [shape(tokens, kv_width)], [own, returned], deps=mine_in[1:3], weight=0)
        grads = gather(lambda k: grad_values)
        factors = [*mine_in, *grads]

        def products(first, last, deps):
            rows = slice(first * sub, last * sub)
            many = (last - first) * sub
            (cross,) = call(functools.partial(product_body, 1, rows), [shape(many, half)], factors, deps=deps)
            (kept,) = call(
                functools.partial(product_body, 0, rows), [shape(many, half, dtype=F32)], factors, deps=deps, weight=3
            )
            return call(
                add_body,
                [shape(sub, half, dtype=BF16 if m else F32) for m in range(first, last)],
                [kept, swap(cross, "dp", 1)],
            )

        far = products(2, len(reduced), [prior_values])
        near = products(0, 2, [far[0]])
        partial = [*near, *far]
        arrived = [away(partial[m], *reduced[m]) for m in (*range(2, len(reduced)), 1)]

    (outgoing,) = call(
        functools.partial(attend_body, blocks),
        [shape(micro, (q_width // LANES) * rows + LABEL_ROWS, LANES)],
        [probs, value_rows, prior_values, plan[0]],
        weight=100,
        deps=[partial[0]] if by_chips else [],
    )
    arrived_out = [outgoing[0]] + [swap(outgoing[m], "dp", m) for m in range(1, micro)]

    token = shape(8, LANES, dtype=F32)
    placed, in_place = call(
        functools.partial(place_body, blocks),
        [shape(tokens, q_width), token],
        arrived_out,
        hbm_out=(0,),
        scratch=[pltpu.VMEM((micro, rows, q_width), BF16), pltpu.SemaphoreType.DMA((micro,))],
        weight=2,
    )
    if by_chips:
        (total,) = call(sum_body, [shape(sub, half)], [partial[0], *arrived], deps=[outgoing])
        sums = [away(total, k // reps, 0, k % reps) for k in reversed(range(1, chips))]
        sums = [total, *reversed(sums)]
        others = {}

        def spread(chosen, so_far=(), weight=0):
            pieces = [sums[k] for k in chosen] + [others[k] for k in chosen]
            return call(
                functools.partial(spread_body, chosen, len(so_far)),
                [shape(chips * sub, kv_width, dtype=F32)] + [token] * (not so_far),
                [*pieces, *so_far],
                weight=weight,
                hbm_in=(len(pieces),),
                hbm_out=(0,),
                scratch=[pltpu.VMEM((len(chosen), sub, kv_width), F32), pltpu.SemaphoreType.DMA((len(chosen),))],
                alias={len(pieces): 0} if so_far else {},
            )

        early = [k for k in range(chips) if k % reps == 0]
        late = [k for k in reversed(range(chips)) if k % reps]
        for k in early:
            others[k] = swap(sums[k], "dp", 1)
        weight_grad, written = spread(early, weight=2)
        for k in late:
            (sums[k],) = call(copy_body, [shape(sub, half)], [sums[k]], deps=[written, in_place])
            others[k] = swap(sums[k], "dp", 1)
        (weight_grad,) = spread(late, [weight_grad])
    else:
        weight_grad = weight_by_collectives(inputs[0], own, returned)
    return (placed[None], weight_grad)


def solution(mesh):
    rows = P("dp", ("ctx", "rep"), None)
    ids = P("dp", ("ctx", "rep"))
    return jax.shard_map(
        local,
        mesh=mesh,
        in_specs=(rows, rows, rows, rows, rows, ids, ids),
        out_specs=(rows, P("ctx", None)),
        check_vma=False,
    )
```

```python
import functools
import math

import jax
import jax.numpy as jnp
from jax import lax
from jax.experimental import pallas as pl
from jax.experimental.pallas import tpu as pltpu
from jax.sharding import PartitionSpec as P

HEAD_DIM = 128
KV_HEADS = 4
GROUP = 4
CORES = 2
LANES = 128
LABEL_ROWS = 16
DOC_BASE = 128
MASKED = -1e30
BF16 = jnp.bfloat16
F32 = jnp.float32


def from_behind(value, axis, by):
    devices = lax.axis_size(axis)
    return lax.ppermute(value, axis, [(i, (i + by) % devices) for i in range(devices)])


def open_ended(value, axis, by):
    devices = lax.axis_size(axis)
    pairs = [(i, i + by) for i in range(devices) if 0 <= i + by < devices]
    return lax.ppermute(value, axis, pairs)


def swap(value, axis, mask):
    devices = lax.axis_size(axis)
    return lax.ppermute(value, axis, [(i, i ^ mask) for i in range(devices)])


def chip_at():
    dp = lax.axis_index("dp")
    return dp % CORES, dp // CORES, lax.axis_index("ctx"), lax.axis_index("rep")


def vmem():
    return pl.BlockSpec(memory_space=pltpu.VMEM)


def smem():
    return pl.BlockSpec(memory_space=pltpu.SMEM)


def call(body, outs, ins, weight=0, deps=(), hbm_in=(), hbm_out=(), scratch=(), alias={}):
    space = pl.BlockSpec(memory_space=pltpu.HBM)
    ins_at = [smem() if a.dtype == jnp.int32 and a.ndim == 1 else vmem() for a in ins]
    ins_at = [space if i in hbm_in else at for i, at in enumerate(ins_at)]
    skip = len(deps)
    ins = [pltpu.with_memory_space_constraint(a, pltpu.HBM) if i in hbm_in else a for i, a in enumerate(ins)]
    return pl.pallas_call(
        lambda *refs: body(*refs[skip:]),
        out_shape=[pltpu.HBM(o.shape, o.dtype) if i in hbm_out else o for i, o in enumerate(outs)],
        in_specs=[space] * skip + ins_at,
        out_specs=[space if i in hbm_out else vmem() for i in range(len(outs))],
        scratch_shapes=list(scratch),
        input_output_aliases={skip + i: o for i, o in alias.items()},
        cost_estimate=pl.CostEstimate(flops=weight * 10**9, bytes_accessed=0, transcendentals=0),
        compiler_params=pltpu.CompilerParams(vmem_limit_bytes=32 * 2**20),
    )(*deps, *ins)


def shape(*dims, dtype=BF16):
    return jax.ShapeDtypeStruct(dims, dtype)


def dot(a, b, dims):
    return lax.dot_general(a, b, (dims, ((), ())), preferred_element_type=F32)


def message_body(key_hbm, doc_hbm, out_ref, doc_ref, sems):
    tokens, width = key_hbm.shape
    copies = [
        pltpu.make_async_copy(doc_hbm, doc_ref, sems.at[0]),
        pltpu.make_async_copy(key_hbm, out_ref.at[pl.ds(0, tokens)], sems.at[1]),
    ]
    for copy in copies:
        copy.start()
    copies[0].wait()
    plus = doc_ref[...] + 1
    high = plus // DOC_BASE
    digits = jnp.concatenate([plus - high * DOC_BASE, high], 1).astype(F32)
    digits = jnp.broadcast_to(digits, (LABEL_ROWS, 2 * tokens)).astype(BF16)
    out_ref[tokens:, : 2 * tokens] = digits
    if width > 2 * tokens:
        out_ref[tokens:, 2 * tokens :] = jnp.zeros((LABEL_ROWS, width - 2 * tokens), BF16)
    copies[1].wait()


def docs_of(message_ref, tokens):
    codes = message_ref[tokens:, : 2 * tokens].astype(F32)[0:1]
    return codes[:, :tokens] + DOC_BASE * codes[:, tokens:] - 1.0


def column_of(row, eye):
    return jnp.sum(jnp.where(eye, row, 0.0), axis=1, keepdims=True)


def probs_body(q_ref, g_ref, k_ref, prior_ref, pt_ref, back_ref):
    tokens = q_ref.shape[0]
    u = lax.broadcasted_iota(jnp.int32, (tokens, tokens), 0)
    t = lax.broadcasted_iota(jnp.int32, (tokens, tokens), 1)
    eye = u == t
    own_docs = docs_of(k_ref, tokens)
    first = (lax.axis_index("ctx") == 0) & (lax.axis_index("rep") == 0)
    prior_docs = jnp.where(first, -1.0, docs_of(prior_ref, tokens))
    prior_ok = column_of(prior_docs, eye) == own_docs
    own_ok = (column_of(own_docs, eye) == own_docs) & (u <= t)
    prior_ok = jnp.concatenate([prior_ok] * GROUP, 1)
    own_ok = jnp.concatenate([own_ok] * GROUP, 1)
    scale = math.log2(math.e) / math.sqrt(HEAD_DIM)
    for g in range(KV_HEADS):
        heads = [slice((g * GROUP + r) * HEAD_DIM, (g * GROUP + r + 1) * HEAD_DIM) for r in range(GROUP)]
        col = slice(g * HEAD_DIM, (g + 1) * HEAD_DIM)
        q4 = jnp.concatenate([q_ref[:, h] for h in heads], 0)
        g4 = jnp.concatenate([g_ref[:, h] for h in heads], 0)
        sp = jnp.where(prior_ok, dot(prior_ref[:tokens, col], q4, ((1,), (1,))), MASKED)
        so = jnp.where(own_ok, dot(k_ref[:tokens, col], q4, ((1,), (1,))), MASKED)
        top = jnp.maximum(jnp.max(sp, 0, keepdims=True), jnp.max(so, 0, keepdims=True))
        ep = jnp.exp2((sp - top) * scale)
        eo = jnp.exp2((so - top) * scale)
        inv = 1.0 / (jnp.sum(ep, 0, keepdims=True) + jnp.sum(eo, 0, keepdims=True))
        pp = (ep * inv).astype(BF16)
        po = (eo * inv).astype(BF16)
        pt_ref[g, :tokens, :] = pp
        pt_ref[g, tokens:, :] = po
        back_ref[:, col] = dot(pp, g4, ((1,), (0,))).astype(BF16)


def own_body(pt_ref, g_ref, own_ref):
    tokens = g_ref.shape[0]
    for g in range(KV_HEADS):
        heads = [slice((g * GROUP + r) * HEAD_DIM, (g * GROUP + r + 1) * HEAD_DIM) for r in range(GROUP)]
        g4 = jnp.concatenate([g_ref[:, h] for h in heads], 0)
        own_ref[:, g * HEAD_DIM : (g + 1) * HEAD_DIM] = dot(pt_ref[g, tokens:, :], g4, ((1,), (0,)))


def copy_body(in_ref, out_ref):
    out_ref[...] = in_ref[...]


def attend_body(blocks, pt_ref, value_ref, prior_ref, plan_ref, out_ref):
    tokens = pt_ref.shape[1] // 2
    rows = tokens // blocks
    owners = out_ref.shape[0]
    data = KV_HEADS * GROUP * rows
    me = lax.axis_index("dp")
    if owners > blocks:
        out_ref[...] = jnp.zeros(out_ref.shape, BF16)
    slots = [plan_ref[j] ^ me for j in range(blocks)]
    for j in range(blocks):
        out_ref[slots[j], data:, :] = jnp.full((LABEL_ROWS, LANES), j + 1, F32).astype(BF16)
    for g in range(KV_HEADS):
        col = slice(g * HEAD_DIM, (g + 1) * HEAD_DIM)
        att = dot(pt_ref[g, :tokens, :], prior_ref[:, col], ((0,), (0,)))
        att = att + dot(pt_ref[g, tokens:, :], value_ref[:, col], ((0,), (0,)))
        att = att.astype(BF16)
        for r in range(GROUP):
            first = (g * GROUP + r) * rows
            for j in range(blocks):
                at = r * tokens + j * rows
                out_ref[slots[j], first : first + rows, :] = att[at : at + rows]


def place_body(blocks, *refs):
    *arrived, out_hbm, done_ref, wide_ref, sems = refs
    done_ref[...] = jnp.zeros(done_ref.shape, F32)
    rows = out_hbm.shape[0] // blocks
    heads = out_hbm.shape[1] // LANES
    labels = [jnp.max(a[heads * rows :, :].astype(F32)).astype(jnp.int32) for a in arrived]
    copies = []
    for i, a in enumerate(arrived):
        first = pl.multiple_of(jnp.maximum(labels[i] - 1, 0) * rows, rows)
        copies.append(pltpu.make_async_copy(wide_ref.at[i], out_hbm.at[pl.ds(first, rows)], sems.at[i]))

        @pl.when(labels[i] > 0)
        def _():
            for h in range(heads):
                wide_ref[i, :, h * LANES : (h + 1) * LANES] = a[h * rows : (h + 1) * rows, :]
            copies[i].start()

    for i, copy in enumerate(copies):

        @pl.when(labels[i] > 0)
        def _():
            copy.wait()


def split_body(reduced, places, chips, in_hbm, q_hbm, g_hbm, v_hbm, *refs):
    spread = len(places)
    outs, (q_ref, g_ref, v_ref, in_ref, sems) = refs[:spread], refs[spread:]
    copies = [
        pltpu.make_async_copy(src, dst, sems.at[i])
        for i, (src, dst) in enumerate(((in_hbm, in_ref), (q_hbm, q_ref), (g_hbm, g_ref), (v_hbm, v_ref)))
    ]
    for copy in copies:
        copy.start()
    sub = in_ref.shape[1] // (spread * len(reduced))
    core, x, z, y = chip_at()
    reps = lax.axis_size("rep")
    copies[0].wait()
    for k, (kx, kz, ky) in enumerate(places):
        for m, (mx, mz, my) in enumerate(reduced):
            first = (z ^ kz ^ mz) * chips + (x ^ kx ^ mx) * reps + (y ^ ky ^ my)
            first = pl.multiple_of(first * sub, sub)
            outs[k][m * sub : (m + 1) * sub, :] = in_ref[:, pl.ds(first, sub)].T
    for copy in copies[1:]:
        copy.wait()


def both_body(own_ref, ret_ref, out_ref):
    out_ref[...] = (own_ref[...] + ret_ref[...].astype(F32)).astype(BF16)


def product_body(cross, rows, *refs):
    *ins, out_ref = refs
    count = len(ins) // 2
    half = out_ref.shape[1]
    core = chip_at()[0] ^ cross
    cols = pl.ds(pl.multiple_of(core * half, half), half)
    a = jnp.concatenate([ref[rows, :] for ref in ins[:count]], 1)
    b = jnp.concatenate([ref[:, cols] for ref in ins[count:]], 0)
    out_ref[...] = dot(a, b, ((1,), (0,))).astype(out_ref.dtype)


def add_body(own_ref, cross_ref, *outs):
    sub = outs[0].shape[0]
    for m, out in enumerate(outs):
        rows = slice(m * sub, (m + 1) * sub)
        out[...] = (own_ref[rows, :] + cross_ref[rows, :].astype(F32)).astype(out.dtype)


def sum_body(*refs):
    *terms, out_ref = refs
    total = terms[0][...]
    for term in terms[1:]:
        total = total + term[...].astype(F32)
    out_ref[...] = total.astype(BF16)


def spread_body(places, resumed, *refs):
    count = len(places)
    mine, other = refs[:count], refs[count : 2 * count]
    *dones, wide_ref, sems = refs[2 * count + resumed :]
    out_hbm, *dones = dones
    for done_ref in dones:
        done_ref[...] = jnp.zeros(done_ref.shape, F32)
    sub, half = mine[0].shape
    core, x, _, y = chip_at()
    q = x * lax.axis_size("rep") + y
    copies = []
    for i, k in enumerate(places):
        for ref, at in ((mine[i], core), (other[i], core ^ 1)):
            wide_ref[i, :, pl.ds(pl.multiple_of(at * half, half), half)] = ref[...].astype(F32)
        rows = pl.ds(pl.multiple_of((q ^ k) * sub, sub), sub)
        copies.append(pltpu.make_async_copy(wide_ref.at[i], out_hbm.at[rows], sems.at[i]))
        copies[i].start()
    for copy in copies:
        copy.wait()


def weight_by_collectives(input_rows, grad_parts):
    own_grad, returned = grad_parts()
    grad_values = (own_grad + returned.astype(F32)).astype(BF16)
    term = jnp.einsum("tc,tf->cf", input_rows, grad_values, preferred_element_type=F32).astype(BF16)
    part = lax.psum_scatter(term, "ctx", scatter_dimension=0, tiled=True).astype(F32)
    return lax.psum(part, ("dp", "rep"))


def weight_by_collectives(input_rows, own_grad, returned):
    grad_values = (own_grad + returned.astype(F32)).astype(BF16)
    term = jnp.einsum("tc,tf->cf", input_rows, grad_values, preferred_element_type=F32).astype(BF16)
    part = lax.psum_scatter(term, "ctx", scatter_dimension=0, tiled=True).astype(F32)
    return lax.psum(part, ("dp", "rep"))


def local(inputs, queries, keys, values, grad_out, doc_ids, plan):
    tokens, width = inputs.shape[1:]
    q_width = queries.shape[2]
    kv_width = keys.shape[2]
    half = kv_width // CORES
    shards = ("ctx", "rep")
    micro, owners, reps = (lax.axis_size(axis) for axis in ("dp", "ctx", "rep"))
    chips = micro // CORES * reps
    blocks = plan.shape[1]
    rows = tokens // blocks

    places = [(kx, kz, 0) for kx in range(micro // CORES) for kz in range(2)]
    reduced = [(0, 2 * mz, my) for mz in range(owners // 2) for my in range(reps)]
    every = ("dp", "ctx", "rep")

    def away(value, x, z, y):
        return swap(value, every, (x * CORES * owners + z) * reps + y)

    sub = width // (len(places) * len(reduced))
    by_chips = sub % LANES == 0

    (message,) = call(
        message_body,
        [shape(tokens + LABEL_ROWS, kv_width)],
        [keys[0], doc_ids],
        hbm_in=(0, 1),
        scratch=[pltpu.VMEM(doc_ids.shape, jnp.int32), pltpu.SemaphoreType.DMA((2,))],
    )
    prior = from_behind(message, shards, 1)

    if by_chips:
        *pieces, q_rows, g_rows, value_rows = call(
            functools.partial(split_body, reduced, places, chips),
            [shape(len(reduced) * sub, tokens)] * len(places) + [shape(tokens, q_width)] * 2 + [shape(tokens, kv_width)],
            [inputs[0], queries[0], grad_out[0], values[0]],
            hbm_in=(0, 1, 2, 3),
            scratch=[pltpu.VMEM((tokens, width), BF16), pltpu.SemaphoreType.DMA((4,))],
        )

        def gather(value_of):
            far_first = [away(value_of(k), *place) for k, place in reversed([*enumerate(places)]) if k]
            x, z = far_first[1:]
            return [far_first[0], z, x, value_of(0)]

        mine_in = gather(lambda k: pieces[k])
    else:
        q_rows, g_rows, value_rows = queries[0], grad_out[0], values[0]

    probs, back = call(
        probs_body,
        [shape(KV_HEADS, 2 * tokens, GROUP * tokens), shape(tokens, kv_width)],
        [q_rows, g_rows, message, prior],
        weight=100,
    )
    (own,) = call(own_body, [shape(tokens, kv_width, dtype=F32)], [probs, g_rows], weight=1)
    returned = from_behind(back, shards, -1)
    prior_values = open_ended(value_rows, shards, 1)
    if by_chips:
        (grad_values,) = call(both_body, [shape(tokens, kv_width)], [own, returned], deps=mine_in[1:3], weight=0)
        grads = gather(lambda k: grad_values)
        factors = [*mine_in, *grads]

        def products(first, last, deps):
            rows = slice(first * sub, last * sub)
            many = (last - first) * sub
            (cross,) = call(functools.partial(product_body, 1, rows), [shape(many, half)], factors, deps=deps)
            (kept,) = call(
                functools.partial(product_body, 0, rows), [shape(many, half, dtype=F32)], factors, deps=deps, weight=3
            )
            return call(
                add_body,
                [shape(sub, half, dtype=BF16 if m else F32) for m in range(first, last)],
                [kept, swap(cross, "dp", 1)],
            )

        far = products(2, len(reduced), [prior_values])
        near = products(0, 2, [far[0]])
        partial = [*near, *far]
        arrived = [away(partial[m], *reduced[m]) for m in (*range(2, len(reduced)), 1)]

    (outgoing,) = call(
        functools.partial(attend_body, blocks),
        [shape(micro, (q_width // LANES) * rows + LABEL_ROWS, LANES)],
        [probs, value_rows, prior_values, plan[0]],
        weight=100,
        deps=[far[0]] if by_chips else [],
    )
    arrived_out = [outgoing[0]] + [swap(outgoing[m], "dp", m) for m in range(1, micro)]

    token = shape(8, LANES, dtype=F32)
    if by_chips:
        (total,) = call(sum_body, [shape(sub, half)], [partial[0], *arrived], deps=[outgoing])

    placed, in_place = call(
        functools.partial(place_body, blocks),
        [shape(tokens, q_width), token],
        arrived_out,
        hbm_out=(0,),
        scratch=[pltpu.VMEM((micro, rows, q_width), BF16), pltpu.SemaphoreType.DMA((micro,))],
        weight=100,
        deps=[total] if by_chips else [],
    )
    if by_chips:
        sums = [away(total, k // reps, 0, k % reps) for k in reversed(range(1, chips))]
        sums = [total, *reversed(sums)]
        others = {}

        def spread(chosen, so_far=(), weight=0):
            pieces = [sums[k] for k in chosen] + [others[k] for k in chosen]
            return call(
                functools.partial(spread_body, chosen, len(so_far)),
                [shape(chips * sub, kv_width, dtype=F32)] + [token] * (not so_far),
                [*pieces, *so_far],
                weight=weight,
                hbm_in=(len(pieces),),
                hbm_out=(0,),
                scratch=[pltpu.VMEM((len(chosen), sub, kv_width), F32), pltpu.SemaphoreType.DMA((len(chosen),))],
                alias={len(pieces): 0} if so_far else {},
            )

        early = [k for k in range(chips) if k % reps == 0]
        late = [k for k in reversed(range(chips)) if k % reps]
        for k in early:
            others[k] = swap(sums[k], "dp", 1)
        weight_grad, written = spread(early, weight=2)
        for k in late:
            (sums[k],) = call(copy_body, [shape(sub, half)], [sums[k]], deps=[written, in_place])
            others[k] = swap(sums[k], "dp", 1)
        (weight_grad,) = spread(late, [weight_grad])
    else:
        weight_grad = weight_by_collectives(inputs[0], own, returned)
    return (placed[None], weight_grad)


def solution(mesh):
    rows = P("dp", ("ctx", "rep"), None)
    ids = P("dp", ("ctx", "rep"))
    return jax.shard_map(
        local,
        mesh=mesh,
        in_specs=(rows, rows, rows, rows, rows, ids, ids),
        out_specs=(rows, P("ctx", None)),
        check_vma=False,
    )
```

```python
import functools
import math

import jax
import jax.numpy as jnp
from jax import lax
from jax.experimental import pallas as pl
from jax.experimental.pallas import tpu as pltpu
from jax.sharding import PartitionSpec as P

HEAD_DIM = 128
KV_HEADS = 4
GROUP = 4
CORES = 2
LANES = 128
LABEL_ROWS = 16
DOC_BASE = 128
MASKED = -1e30
BF16 = jnp.bfloat16
F32 = jnp.float32


def from_behind(value, axis, by):
    devices = lax.axis_size(axis)
    return lax.ppermute(value, axis, [(i, (i + by) % devices) for i in range(devices)])


def open_ended(value, axis, by):
    devices = lax.axis_size(axis)
    pairs = [(i, i + by) for i in range(devices) if 0 <= i + by < devices]
    return lax.ppermute(value, axis, pairs)


def swap(value, axis, mask):
    devices = lax.axis_size(axis)
    return lax.ppermute(value, axis, [(i, i ^ mask) for i in range(devices)])


def chip_at():
    dp = lax.axis_index("dp")
    return dp % CORES, dp // CORES, lax.axis_index("ctx"), lax.axis_index("rep")


def vmem():
    return pl.BlockSpec(memory_space=pltpu.VMEM)


def smem():
    return pl.BlockSpec(memory_space=pltpu.SMEM)


def call(body, outs, ins, weight=0, deps=(), hbm_in=(), hbm_out=(), scratch=(), alias={}):
    space = pl.BlockSpec(memory_space=pltpu.HBM)
    ins_at = [smem() if a.dtype == jnp.int32 and a.ndim == 1 else vmem() for a in ins]
    ins_at = [space if i in hbm_in else at for i, at in enumerate(ins_at)]
    skip = len(deps)
    ins = [pltpu.with_memory_space_constraint(a, pltpu.HBM) if i in hbm_in else a for i, a in enumerate(ins)]
    return pl.pallas_call(
        lambda *refs: body(*refs[skip:]),
        out_shape=[pltpu.HBM(o.shape, o.dtype) if i in hbm_out else o for i, o in enumerate(outs)],
        in_specs=[space] * skip + ins_at,
        out_specs=[space if i in hbm_out else vmem() for i in range(len(outs))],
        scratch_shapes=list(scratch),
        input_output_aliases={skip + i: o for i, o in alias.items()},
        cost_estimate=pl.CostEstimate(flops=weight * 10**9, bytes_accessed=0, transcendentals=0),
        compiler_params=pltpu.CompilerParams(vmem_limit_bytes=32 * 2**20),
    )(*deps, *ins)


def shape(*dims, dtype=BF16):
    return jax.ShapeDtypeStruct(dims, dtype)


def dot(a, b, dims):
    return lax.dot_general(a, b, (dims, ((), ())), preferred_element_type=F32)


def message_body(key_hbm, doc_hbm, out_ref, doc_ref, sems):
    tokens = key_hbm.shape[0]
    copies = [pltpu.make_async_copy(doc_hbm, doc_ref, sems.at[KV_HEADS])]
    for g in range(KV_HEADS):
        head = key_hbm.at[:, pl.ds(g * HEAD_DIM, HEAD_DIM)]
        copies.append(pltpu.make_async_copy(head, out_ref.at[pl.ds(g * tokens, tokens)], sems.at[g]))
    for copy in copies:
        copy.start()
    copies[0].wait()
    plus = doc_ref[...] + 1
    high = plus // DOC_BASE
    row = lax.broadcasted_iota(jnp.int32, (LABEL_ROWS, tokens), 0)
    digits = jnp.where(row == 0, plus - high * DOC_BASE, high)
    out_ref[KV_HEADS * tokens :, :] = digits.astype(F32).astype(BF16)
    for copy in copies[1:]:
        copy.wait()


def docs_of(message_ref, tokens):
    codes = message_ref[KV_HEADS * tokens :, :].astype(F32)
    return codes[0:1] + DOC_BASE * codes[1:2] - 1.0


def column_of(row, eye):
    return jnp.sum(jnp.where(eye, row, 0.0), axis=1, keepdims=True)


def probs_body(q_ref, g_ref, k_ref, prior_ref, pt_ref, back_ref):
    tokens = q_ref.shape[0]
    u = lax.broadcasted_iota(jnp.int32, (tokens, tokens), 0)
    t = lax.broadcasted_iota(jnp.int32, (tokens, tokens), 1)
    eye = u == t
    own_docs = docs_of(k_ref, tokens)
    first = (lax.axis_index("ctx") == 0) & (lax.axis_index("rep") == 0)
    prior_docs = jnp.where(first, -1.0, docs_of(prior_ref, tokens))
    prior_ok = column_of(prior_docs, eye) == own_docs
    own_ok = (column_of(own_docs, eye) == own_docs) & (u <= t)
    prior_ok = jnp.concatenate([prior_ok] * GROUP, 1)
    own_ok = jnp.concatenate([own_ok] * GROUP, 1)
    scale = math.log2(math.e) / math.sqrt(HEAD_DIM)
    for g in range(KV_HEADS):
        heads = [slice((g * GROUP + r) * HEAD_DIM, (g * GROUP + r + 1) * HEAD_DIM) for r in range(GROUP)]
        col = slice(g * HEAD_DIM, (g + 1) * HEAD_DIM)
        below = slice(g * tokens, (g + 1) * tokens)
        q4 = jnp.concatenate([q_ref[:, h] for h in heads], 0)
        g4 = jnp.concatenate([g_ref[:, h] for h in heads], 0)
        sp = jnp.where(prior_ok, dot(prior_ref[below, :], q4, ((1,), (1,))), MASKED)
        so = jnp.where(own_ok, dot(k_ref[below, :], q4, ((1,), (1,))), MASKED)
        top = jnp.maximum(jnp.max(sp, 0, keepdims=True), jnp.max(so, 0, keepdims=True))
        ep = jnp.exp2((sp - top) * scale)
        eo = jnp.exp2((so - top) * scale)
        inv = 1.0 / (jnp.sum(ep, 0, keepdims=True) + jnp.sum(eo, 0, keepdims=True))
        pp = (ep * inv).astype(BF16)
        po = (eo * inv).astype(BF16)
        pt_ref[g, :tokens, :] = pp
        pt_ref[g, tokens:, :] = po
        back_ref[:, col] = dot(pp, g4, ((1,), (0,))).astype(BF16)


def own_body(pt_ref, g_ref, own_ref):
    tokens = g_ref.shape[0]
    for g in range(KV_HEADS):
        heads = [slice((g * GROUP + r) * HEAD_DIM, (g * GROUP + r + 1) * HEAD_DIM) for r in range(GROUP)]
        g4 = jnp.concatenate([g_ref[:, h] for h in heads], 0)
        own_ref[:, g * HEAD_DIM : (g + 1) * HEAD_DIM] = dot(pt_ref[g, tokens:, :], g4, ((1,), (0,)))


def copy_body(in_ref, out_ref):
    out_ref[...] = in_ref[...]


def attend_body(blocks, pt_ref, value_ref, prior_ref, plan_ref, out_ref):
    tokens = pt_ref.shape[1] // 2
    rows = tokens // blocks
    owners = out_ref.shape[0]
    data = KV_HEADS * GROUP * rows
    me = lax.axis_index("dp")
    if owners > blocks:
        out_ref[...] = jnp.zeros(out_ref.shape, BF16)
    slots = [plan_ref[j] ^ me for j in range(blocks)]
    for j in range(blocks):
        out_ref[slots[j], data:, :] = jnp.full((LABEL_ROWS, LANES), j + 1, F32).astype(BF16)
    for g in range(KV_HEADS):
        col = slice(g * HEAD_DIM, (g + 1) * HEAD_DIM)
        att = dot(pt_ref[g, :tokens, :], prior_ref[:, col], ((0,), (0,)))
        att = att + dot(pt_ref[g, tokens:, :], value_ref[:, col], ((0,), (0,)))
        att = att.astype(BF16)
        for r in range(GROUP):
            first = (g * GROUP + r) * rows
            for j in range(blocks):
                at = r * tokens + j * rows
                out_ref[slots[j], first : first + rows, :] = att[at : at + rows]


def place_body(blocks, *refs):
    *arrived, out_hbm, done_ref, wide_ref, sems = refs
    done_ref[...] = jnp.zeros(done_ref.shape, F32)
    rows = out_hbm.shape[0] // blocks
    heads = out_hbm.shape[1] // LANES
    labels = [jnp.max(a[heads * rows :, :].astype(F32)).astype(jnp.int32) for a in arrived]
    copies = []
    for i, a in enumerate(arrived):
        first = pl.multiple_of(jnp.maximum(labels[i] - 1, 0) * rows, rows)
        copies.append(pltpu.make_async_copy(wide_ref.at[i], out_hbm.at[pl.ds(first, rows)], sems.at[i]))

        @pl.when(labels[i] > 0)
        def _():
            for h in range(heads):
                wide_ref[i, :, h * LANES : (h + 1) * LANES] = a[h * rows : (h + 1) * rows, :]
            copies[i].start()

    for i, copy in enumerate(copies):

        @pl.when(labels[i] > 0)
        def _():
            copy.wait()


def split_body(reduced, places, chips, in_hbm, q_hbm, g_hbm, v_hbm, *refs):
    spread = len(places)
    outs, (q_ref, g_ref, v_ref, in_ref, sems) = refs[:spread], refs[spread:]
    copies = [
        pltpu.make_async_copy(src, dst, sems.at[i])
        for i, (src, dst) in enumerate(((in_hbm, in_ref), (q_hbm, q_ref), (g_hbm, g_ref), (v_hbm, v_ref)))
    ]
    for copy in copies:
        copy.start()
    sub = in_ref.shape[1] // (spread * len(reduced))
    core, x, z, y = chip_at()
    reps = lax.axis_size("rep")
    copies[0].wait()
    for k, (kx, kz, ky) in enumerate(places):
        for m, (mx, mz, my) in enumerate(reduced):
            first = (z ^ kz ^ mz) * chips + (x ^ kx ^ mx) * reps + (y ^ ky ^ my)
            first = pl.multiple_of(first * sub, sub)
            outs[k][m * sub : (m + 1) * sub, :] = in_ref[:, pl.ds(first, sub)].T
    for copy in copies[1:]:
        copy.wait()


def both_body(own_ref, ret_ref, out_ref):
    out_ref[...] = (own_ref[...] + ret_ref[...].astype(F32)).astype(BF16)


def product_body(cross, rows, *refs):
    *ins, out_ref = refs
    count = len(ins) // 2
    half = out_ref.shape[1]
    core = chip_at()[0] ^ cross
    cols = pl.ds(pl.multiple_of(core * half, half), half)
    a = jnp.concatenate([ref[rows, :] for ref in ins[:count]], 1)
    b = jnp.concatenate([ref[:, cols] for ref in ins[count:]], 0)
    out_ref[...] = dot(a, b, ((1,), (0,))).astype(out_ref.dtype)


def add_body(own_ref, cross_ref, *outs):
    sub = outs[0].shape[0]
    for m, out in enumerate(outs):
        rows = slice(m * sub, (m + 1) * sub)
        out[...] = (own_ref[rows, :] + cross_ref[rows, :].astype(F32)).astype(out.dtype)


def sum_body(*refs):
    *terms, out_ref = refs
    total = terms[0][...]
    for term in terms[1:]:
        total = total + term[...].astype(F32)
    out_ref[...] = total.astype(BF16)


def spread_body(places, resumed, *refs):
    count = len(places)
    mine, other = refs[:count], refs[count : 2 * count]
    *dones, wide_ref, sems = refs[2 * count + resumed :]
    out_hbm, *dones = dones
    for done_ref in dones:
        done_ref[...] = jnp.zeros(done_ref.shape, F32)
    sub, half = mine[0].shape
    core, x, _, y = chip_at()
    q = x * lax.axis_size("rep") + y
    copies = []
    for i, k in enumerate(places):
        for ref, at in ((mine[i], core), (other[i], core ^ 1)):
            wide_ref[i, :, pl.ds(pl.multiple_of(at * half, half), half)] = ref[...].astype(F32)
        rows = pl.ds(pl.multiple_of((q ^ k) * sub, sub), sub)
        copies.append(pltpu.make_async_copy(wide_ref.at[i], out_hbm.at[rows], sems.at[i]))
        copies[i].start()
    for copy in copies:
        copy.wait()


def weight_by_collectives(input_rows, grad_parts):
    own_grad, returned = grad_parts()
    grad_values = (own_grad + returned.astype(F32)).astype(BF16)
    term = jnp.einsum("tc,tf->cf", input_rows, grad_values, preferred_element_type=F32).astype(BF16)
    part = lax.psum_scatter(term, "ctx", scatter_dimension=0, tiled=True).astype(F32)
    return lax.psum(part, ("dp", "rep"))


def weight_by_collectives(input_rows, own_grad, returned):
    grad_values = (own_grad + returned.astype(F32)).astype(BF16)
    term = jnp.einsum("tc,tf->cf", input_rows, grad_values, preferred_element_type=F32).astype(BF16)
    part = lax.psum_scatter(term, "ctx", scatter_dimension=0, tiled=True).astype(F32)
    return lax.psum(part, ("dp", "rep"))


def local(inputs, queries, keys, values, grad_out, doc_ids, plan):
    tokens, width = inputs.shape[1:]
    q_width = queries.shape[2]
    kv_width = keys.shape[2]
    half = kv_width // CORES
    shards = ("ctx", "rep")
    micro, owners, reps = (lax.axis_size(axis) for axis in ("dp", "ctx", "rep"))
    chips = micro // CORES * reps
    blocks = plan.shape[1]
    rows = tokens // blocks

    places = [(kx, kz, 0) for kx in range(micro // CORES) for kz in range(2)]
    reduced = [(0, 2 * mz, my) for mz in range(owners // 2) for my in range(reps)]
    every = ("dp", "ctx", "rep")

    def away(value, x, z, y):
        return swap(value, every, (x * CORES * owners + z) * reps + y)

    sub = width // (len(places) * len(reduced))
    by_chips = sub % LANES == 0

    (message,) = call(
        message_body,
        [shape(KV_HEADS * tokens + LABEL_ROWS, HEAD_DIM)],
        [keys[0], doc_ids],
        hbm_in=(0, 1),
        scratch=[pltpu.VMEM(doc_ids.shape, jnp.int32), pltpu.SemaphoreType.DMA((KV_HEADS + 1,))],
    )
    prior = from_behind(message, shards, 1)

    if by_chips:
        *pieces, q_rows, g_rows, value_rows = call(
            functools.partial(split_body, reduced, places, chips),
            [shape(len(reduced) * sub, tokens)] * len(places) + [shape(tokens, q_width)] * 2 + [shape(tokens, kv_width)],
            [inputs[0], queries[0], grad_out[0], values[0]],
            hbm_in=(0, 1, 2, 3),
            scratch=[pltpu.VMEM((tokens, width), BF16), pltpu.SemaphoreType.DMA((4,))],
        )

        def gather(value_of):
            far_first = [away(value_of(k), *place) for k, place in reversed([*enumerate(places)]) if k]
            x, z = far_first[1:]
            return [far_first[0], z, x, value_of(0)]

        mine_in = gather(lambda k: pieces[k])
    else:
        q_rows, g_rows, value_rows = queries[0], grad_out[0], values[0]

    probs, back = call(
        probs_body,
        [shape(KV_HEADS, 2 * tokens, GROUP * tokens), shape(tokens, kv_width)],
        [q_rows, g_rows, message, prior],
        weight=100,
    )
    (own,) = call(own_body, [shape(tokens, kv_width, dtype=F32)], [probs, g_rows], weight=1)
    returned = from_behind(back, shards, -1)
    prior_values = open_ended(value_rows, shards, 1)
    if by_chips:
        (grad_values,) = call(both_body, [shape(tokens, kv_width)], [own, returned], deps=mine_in[1:3], weight=0)
        grads = gather(lambda k: grad_values)
        factors = [*mine_in, *grads]

        def products(first, last, deps):
            rows = slice(first * sub, last * sub)
            many = (last - first) * sub
            (cross,) = call(functools.partial(product_body, 1, rows), [shape(many, half)], factors, deps=deps)
            (kept,) = call(
                functools.partial(product_body, 0, rows), [shape(many, half, dtype=F32)], factors, deps=deps, weight=3
            )
            return call(
                add_body,
                [shape(sub, half, dtype=BF16 if m else F32) for m in range(first, last)],
                [kept, swap(cross, "dp", 1)],
            )

        far = products(2, len(reduced), [prior_values])
        near = products(0, 2, [far[0]])
        partial = [*near, *far]
        arrived = [away(partial[m], *reduced[m]) for m in (*range(2, len(reduced)), 1)]

    (outgoing,) = call(
        functools.partial(attend_body, blocks),
        [shape(micro, (q_width // LANES) * rows + LABEL_ROWS, LANES)],
        [probs, value_rows, prior_values, plan[0]],
        weight=100,
        deps=[far[0]] if by_chips else [],
    )
    arrived_out = [outgoing[0]] + [swap(outgoing[m], "dp", m) for m in range(1, micro)]

    token = shape(8, LANES, dtype=F32)
    if by_chips:
        (total,) = call(sum_body, [shape(sub, half)], [partial[0], *arrived], deps=[outgoing])

    placed, in_place = call(
        functools.partial(place_body, blocks),
        [shape(tokens, q_width), token],
        arrived_out,
        hbm_out=(0,),
        scratch=[pltpu.VMEM((micro, rows, q_width), BF16), pltpu.SemaphoreType.DMA((micro,))],
        weight=100,
        deps=[total] if by_chips else [],
    )
    if by_chips:
        sums = [away(total, k // reps, 0, k % reps) for k in reversed(range(1, chips))]
        sums = [total, *reversed(sums)]
        others = {}

        def spread(chosen, so_far=(), weight=0):
            pieces = [sums[k] for k in chosen] + [others[k] for k in chosen]
            return call(
                functools.partial(spread_body, chosen, len(so_far)),
                [shape(chips * sub, kv_width, dtype=F32)] + [token] * (not so_far),
                [*pieces, *so_far],
                weight=weight,
                hbm_in=(len(pieces),),
                hbm_out=(0,),
                scratch=[pltpu.VMEM((len(chosen), sub, kv_width), F32), pltpu.SemaphoreType.DMA((len(chosen),))],
                alias={len(pieces): 0} if so_far else {},
            )

        early = [k for k in range(chips) if k % reps == 0]
        late = [k for k in reversed(range(chips)) if k % reps]
        for k in early:
            others[k] = swap(sums[k], "dp", 1)
        weight_grad, written = spread(early, weight=2)
        for k in late:
            (sums[k],) = call(copy_body, [shape(sub, half)], [sums[k]], deps=[written, in_place])
            others[k] = swap(sums[k], "dp", 1)
        (weight_grad,) = spread(late, [weight_grad])
    else:
        weight_grad = weight_by_collectives(inputs[0], own, returned)
    return (placed[None], weight_grad)


def solution(mesh):
    rows = P("dp", ("ctx", "rep"), None)
    ids = P("dp", ("ctx", "rep"))
    return jax.shard_map(
        local,
        mesh=mesh,
        in_specs=(rows, rows, rows, rows, rows, ids, ids),
        out_specs=(rows, P("ctx", None)),
        check_vma=False,
    )
```
